512 devices in a mesh: expert: 8 (over y), dp: 64 (over z, x, core).
Axes of the slice: x: 4, y: 8, z: 8, core: 2. Of those that a mesh axis runs over, the one named last changes fastest.
Arguments:
- tokens: bfloat16 [16384, 2080], P('dp')
- grad_out: bfloat16 [16384, 3072], P('dp', 'expert')
- counts: int32 [64], P('dp'), may hold values from 8 to 256, as said below
- weight: bfloat16 [3072, 2080], P(('expert', 'dp')), may hold values from -3 to 3
- row_state: float32 [3072], P(('expert', 'dp')), may hold values from 0.01 to 0.75
- col_state: float32 [2080], replicated, may hold values from 0.05 to 0.5
Outputs:
- new_weight: bfloat16 [3072, 2080], P(('expert', 'dp'))
- new_rows: float32 [3072], P(('expert', 'dp'))
- new_cols: float32 [2080], replicated
The draws below stay inside these ranges and needn't reach their ends.
Inputs may be any that keep to these rules, and one draw needn't show every extreme that they name: `counts`: each count is a multiple of 8; some index of dp has all 256 slots live in every draw.
All inputs are finite; a program needn't handle non-finite values.
Results may differ from the reference program's by a relative error of at most 0.001.
Values sent between devices are 32-bit elements; how exact they have to be, the bound alone decides.
A program may use at most 64 MiB of HBM per device.

```python
import math
import jax
import jax.numpy as jnp
from jax import lax

D = 2080
FFW = 3072
CAP = 256
TOKENS = 16384
N_DP = 64


def spread(key, values, base):
    first, second = jax.random.split(key)
    row_scale = jnp.exp(jax.random.uniform(first, (values.shape[0], 1), minval=0.0, maxval=2.3))
    col_scale = jnp.exp(jax.random.uniform(second, (1, values.shape[1]), minval=0.0, maxval=2.3))
    return base * values * row_scale * col_scale


def draw_tokens(key, part):
    key = jax.random.fold_in(key, 11)
    first, second = jax.random.split(key, 2)
    values = jax.random.normal(first, (TOKENS, D))
    return spread(second, values, 1.0).astype(jnp.bfloat16)


def draw_grad_out(key, part):
    key = jax.random.fold_in(key, 12)
    first, second = jax.random.split(key, 2)
    values = jax.random.normal(first, (TOKENS, FFW))
    base = 0.0068 / TOKENS ** 0.5
    return spread(second, values, base).astype(jnp.bfloat16)


def draw_counts(key, part):
    key = jax.random.fold_in(key, 13)
    first, second, third = jax.random.split(key, 3)
    blocks = CAP // 8
    one_draw = jax.random.randint(first, (N_DP,), 1, blocks + 1)
    two_draw = jax.random.randint(second, (N_DP,), 1, blocks + 1)
    tiles = jnp.minimum(one_draw, two_draw)
    fullest = jax.random.randint(third, (), 0, N_DP)
    tiles = jnp.where(jnp.arange(N_DP, dtype=jnp.int32) == fullest, blocks, tiles)
    return (tiles * 8).astype(jnp.int32)


def trend_rows(key, ratio):
    position = jnp.arange(FFW, dtype=jnp.float32) / FFW
    factor = jax.random.uniform(key, (FFW,), minval=1.0, maxval=1.5)
    return 0.5 * jnp.exp(-jnp.log(ratio) * position) * factor


def draw_row_state(key, part):
    key = jax.random.fold_in(key, 14)
    values = trend_rows(key, 10.0)
    return values.astype(jnp.float32)


def level_of(own_key, extent, cuts, low, top_value):
    def one(dim, parts):
        draws = jax.random.uniform(jax.random.fold_in(jax.random.fold_in(own_key, 6), dim), (parts,), jnp.float32, low / len(cuts), top_value / len(cuts))
        return jnp.repeat(jnp.exp(draws), extent[dim] // parts).reshape((-1,) + (1,) * (len(extent) - dim - 1))

    level = one(*cuts[0])
    for cut in cuts[1:]:
        level = level * one(*cut)
    return level


def centred(rng, dims, scale, reach, pieces=(), kind=jnp.bfloat16):
    factor_of = level_of(rng, dims, pieces, -0.22, 0.18) if pieces else 1.0
    entries = jax.random.normal(rng, dims, jnp.float32) * scale * factor_of
    return jnp.minimum(jnp.maximum(entries, -reach), reach).astype(kind)


def setup_inputs(seed: int = 0) -> dict:
    keys = jax.random.split(jax.random.key(seed), 7)
    tokens = draw_tokens(jax.random.fold_in(keys[6], 71), 0)
    grad_out = draw_grad_out(jax.random.fold_in(keys[6], 71), 0)
    counts = draw_counts(jax.random.fold_in(keys[6], 71), 0)
    weight = centred(keys[3], (FFW, D), 0.5, 3.0, ((0, 512),))
    row_state = draw_row_state(jax.random.fold_in(keys[6], 71), 0)
    col_state = jnp.clip(jnp.exp(jax.random.uniform(keys[5], (D,), jnp.float32, math.log(0.05), math.log(0.5))), 0.05, 0.5)
    return {"tokens": tokens, "grad_out": grad_out, "counts": counts, "weight": weight, "row_state": row_state, "col_state": col_state}


def reference(tokens, grad_out, counts, weight, row_state, col_state):
    index = jnp.arange(TOKENS, dtype=jnp.int32)
    limits = jnp.repeat(counts, CAP, total_repeat_length=TOKENS)
    live = index % CAP < limits
    masked = jnp.where(live[:, None], grad_out, jnp.zeros_like(grad_out))
    grad = jnp.dot(masked.T, tokens, preferred_element_type=jnp.float32)
    squared = grad * grad
    row_mean = lax.optimization_barrier(jnp.mean(squared, axis=1)) + 1e-06
    new_rows = 0.5 * row_state + 0.5 * row_mean
    col_mean = lax.optimization_barrier(jnp.mean(squared, axis=0)) + 1e-06
    new_cols = 0.5 * col_state + 0.5 * col_mean
    row_avg = jnp.mean(new_rows)
    update = grad / jnp.sqrt(new_rows[:, None] * new_cols[None, :] / row_avg)
    rms_value = jnp.sqrt(jnp.mean(update * update))
    scaled = update / jnp.maximum(1.0, rms_value)
    new_weight = (weight.astype(jnp.float32) - 0.1 * scaled).astype(jnp.bfloat16)
    return (new_weight, new_rows, new_cols)
```

```python
import jax
import jax.numpy as jnp
import numpy as np
from jax import lax
from jax.experimental import pallas as pl
from jax.experimental.pallas import tpu as pltpu
from jax.sharding import PartitionSpec as P

D = 2080
FFW = 3072
NY, NZ, NX, NC = 8, 8, 4, 2
OWN = 6
ROWS = NC * OWN
WIDE = 1024
PART = 16
HALF = WIDE + 128
MESH = pl.DeviceIdType.MESH
F32 = jnp.float32


def row_order():
    pick = np.zeros((384, 384), np.float32)
    for x in range(NX):
        for z in range(NZ):
            for k in range(ROWS):
                pick[(x * NZ + z) * ROWS + k, (z * NX + x) * ROWS + k] = 1
    return pick


def kernel(
    tok_ref, go_ref, cnt_ref, w_ref, rs_ref, cs_ref, pick_ref,
    nw_ref, nr_ref, nc_ref,
    tok2, lhs, other, acc, core_in, d2_in, d1_in, z_in, g_own, g_sib, r_own, r_sib,
    st_y, st_z, st_x, st_sum, st_sib, wide, gwide,
    core_s, core_r, d2_s, d2_r, d1_s, d1_r, zs, zr, gs, gr, ys, yr, z2s, z2r, xs, xr,
):
    e = lax.axis_index("expert")
    q = lax.axis_index("dp")
    c, x, z = q % 2, (q // 2) % NX, q // (2 * NX)

    def at(ee, zz, xx, cc):
        return (ee, (zz * NX + xx) * 2 + cc)

    sib = at(e, z, x, 1 - c)
    y_peers = [at((e + d) % NY, z, x, c) for d in range(1, NY)]
    z_peers = [at(e, (z + d) % NZ, x, c) for d in range(1, NZ)]
    x_peers = [at(e, z, (x + d) % NX, c) for d in range(1, NX)]
    right, left = x_peers[0], x_peers[2]

    barrier = pltpu.get_barrier_semaphore()
    everyone = [sib] + y_peers + z_peers + x_peers
    for peer in everyone:
        pl.semaphore_signal(barrier, inc=1, device_id=peer, device_id_type=MESH)

    def remote(src, dst, s, r, peer):
        return pltpu.make_async_remote_copy(
            src_ref=src, dst_ref=dst, send_sem=s, recv_sem=r, device_id=peer, device_id_type=MESH
        )

    live = lax.broadcasted_iota(jnp.int32, (256, 384), 0) < cnt_ref[0]
    masked = jnp.where(live, go_ref[...].astype(F32), 0.0).astype(jnp.bfloat16)
    lhs[...] = lax.dot_general(
        pick_ref[...], masked, (((1,), (1,)), ((), ())), preferred_element_type=F32
    ).astype(jnp.bfloat16).reshape(NX, 96, 256)
    tail = tok_ref[:, 2 * WIDE : D]
    for h in range(2):
        tok2[h, :, 0:WIDE] = tok_ref[:, h * WIDE : (h + 1) * WIDE]
        put = lax.broadcasted_iota(jnp.int32, (32, 128), 0) == lax.broadcasted_iota(jnp.int32, (32, 128), 1) + h * PART
        put &= lax.broadcasted_iota(jnp.int32, (32, 128), 1) < PART
        put = jnp.where(put, 1.0, 0.0).astype(jnp.bfloat16)
        tok2[h, :, WIDE:HALF] = jnp.dot(tail, put, preferred_element_type=F32).astype(jnp.bfloat16)

    def product(k, _):
        block = lhs[k]
        other[k] = jnp.dot(block, tok2[1 - c], preferred_element_type=F32).reshape(4, 24, HALF)
        acc[k] = jnp.dot(block, tok2[c], preferred_element_type=F32).reshape(4, 24, HALF)
        return 0

    lax.fori_loop(0, NX, product, 0)
    pl.semaphore_wait(barrier, len(everyone))

    slabs = [(x + 2) % NX, (x + 1) % NX, (x + 3) % NX, x]
    core = [remote(other.at[k], core_in.at[k], core_s.at[j], core_r.at[j], sib) for j, k in enumerate(slabs)]
    for cp in core:
        cp.start()

    def settle(j):
        core[j].wait_recv()
        acc[slabs[j]] += core_in[slabs[j]]

    pz = z // 2
    far, up, down = (pz + 2) % 4, (pz + 1) % 4, (pz + 3) % 4
    settle(0)
    started = []
    d2 = {}
    for side, peer, chunks in ((0, right, (far, down)), (1, left, (up, pz))):
        for i, p in enumerate(chunks):
            cp = remote(acc.at[slabs[0], p], d2_in.at[side, i], d2_s.at[side, i], d2_r.at[side, i], peer)
            cp.start()
            d2[side, i] = cp
            started.append(cp)
    d1 = {}

    def forward(side, i, p, merge):
        k = slabs[1 + side]
        if merge is not None:
            d2[side, merge].wait_recv()
            acc[k, p] += d2_in[side, merge]
        cp = remote(acc.at[k, p], d1_in.at[side, i], d1_s.at[side, i], d1_r.at[side, i], (right, left)[side])
        cp.start()
        d1[side, i] = cp
        started.append(cp)

    settle(1)
    forward(0, 0, up, None)
    settle(2)
    forward(1, 0, far, None)
    settle(3)
    forward(0, 1, far, 0)
    forward(1, 1, up, 0)
    forward(0, 2, pz, None)
    forward(1, 2, down, None)
    forward(0, 3, down, 1)
    forward(1, 3, pz, 1)

    h0 = z % 2

    def collect(p, i, j):
        d1[0, i].wait_recv()
        d1[1, j].wait_recv()
        acc[x, p] += d1_in[0, i] + d1_in[1, j]

    def deliver(p, h):
        to = 2 * p + h
        first = pl.multiple_of(8 * h, 8)
        cp = remote(acc.at[x, p, pl.ds(first, 16)], z_in.at[z], zs.at[to], zr.at[z], at(e, to, x, c))
        cp.start()
        started.append(cp)

    collect(far, 1, 0)
    deliver(far, 0)
    deliver(far, 1)
    collect(up, 0, 1)
    deliver(up, 0)
    deliver(up, 1)
    collect(pz, 2, 3)
    deliver(pz, 1 - h0)
    collect(down, 3, 2)
    deliver(down, 0)
    deliver(down, 1)
    total = acc[x, pz, pl.ds(pl.multiple_of(8 * h0, 8), 16), :]
    for d in (4, 3, 5, 2, 6, 7, 1):
        k = (z + d) % NZ
        remote(z_in.at[k], z_in.at[k], zs.at[k], zr.at[k], sib).wait_recv()
        total += z_in[k]
    moved = jnp.concatenate([total[4:16], total[0:4]], axis=0)
    row16 = lax.broadcasted_iota(jnp.int32, (16, 1), 0)
    grad = jnp.where(row16 < ROWS, jnp.where(h0 == 1, moved, total), 0.0)
    g_own[...] = grad

    squared = grad * grad
    lane = lax.broadcasted_iota(jnp.int32, (16, 128), 1)
    row = lax.broadcasted_iota(jnp.int32, (16, 128), 0)
    state = jnp.zeros((16, 128), F32)
    for k in range(OWN):
        state = jnp.where(row == c * OWN + k, rs_ref[k], state)
    r_own[...] = jnp.where(lane < 64, jnp.sum(squared, axis=1, keepdims=True), state)
    r_copy = remote(r_own, r_sib, gs.at[0], gr.at[0], sib)
    r_copy.start()
    g_copy = remote(g_own, g_sib, gs.at[1], gr.at[1], sib)
    g_copy.start()
    started += [r_copy, g_copy]
    col_part = jnp.sum(squared, axis=0, keepdims=True)
    r_copy.wait_recv()
    both = r_own[...] + r_sib[...]
    new_rows = 0.5 * both[:, 64:65] + 0.5 * (both[:, 0:1] / D + 1e-06)
    s_part = jnp.sum(squared / new_rows, axis=0, keepdims=True)
    row_part = jnp.sum(jnp.where(row16 < ROWS, new_rows, 0.0), axis=0, keepdims=True)

    for k in range(9):
        st_y[e, k : k + 1, :] = col_part[:, 128 * k : 128 * (k + 1)]
        st_y[e, 9 + k : 10 + k, :] = s_part[:, 128 * k : 128 * (k + 1)]
    st_y[e, 18:24, :] = jnp.broadcast_to(row_part, (6, 128))

    def exchange(buf, me, n, s, r, peers):
        for d in range(1, n):
            cp = remote(buf.at[me], buf.at[me], s.at[d], r.at[me], peers[d - 1])
            cp.start()
            started.append(cp)
        for d in range(1, n):
            k = (me + d) % n
            remote(buf.at[k], buf.at[k], s.at[0], r.at[k], sib).wait_recv()
        out = buf[0]
        for k in range(1, n):
            out += buf[k]
        return out

    st_z[z] = exchange(st_y, e, NY, ys, yr, y_peers)
    st_x[x] = exchange(st_z, z, NZ, z2s, z2r, z_peers)
    mine = exchange(st_x, x, NX, xs, xr, x_peers)
    st_sum[...] = mine
    last = remote(st_sum, st_sib, gs.at[2], gr.at[2], sib)
    last.start()
    started.append(last)

    def halves(own, sibling):
        return jnp.where(c == 0, own, sibling), jnp.where(c == 0, sibling, own)

    g_copy.wait_recv()
    picked = []
    for ref in (g_own, g_sib):
        v = ref[...]
        picked.append(jnp.where(c == 0, v[0:8], jnp.concatenate([v[6:14]], axis=0)))
    first, second = halves(*picked)
    gwide[:, 0:WIDE] = first[:, 0:WIDE]
    gwide[:, WIDE : 2 * WIDE] = second[:, 0:WIDE]
    gwide[:, 2 * WIDE :] = first[:, WIDE:] + pltpu.roll(second[:, WIDE:], PART, 1)
    rows8 = jnp.where(c == 0, new_rows[0:8], new_rows[6:14])
    eye = lax.broadcasted_iota(jnp.int32, (8, 128), 0) == lax.broadcasted_iota(jnp.int32, (8, 128), 1)
    nr_ref[...] = jnp.sum(jnp.where(eye, rows8, 0.0), axis=0)[0:OWN]

    last.wait_recv()
    first, second = halves(mine, st_sib[...])
    for k in range(8):
        for j in range(2):
            wide[j : j + 1, 128 * k : 128 * (k + 1)] = first[9 * j + k : 9 * j + k + 1]
            wide[j : j + 1, WIDE + 128 * k : WIDE + 128 * (k + 1)] = second[9 * j + k : 9 * j + k + 1]
    for j in range(2):
        wide[j : j + 1, 2 * WIDE :] = first[9 * j + 8 : 9 * j + 9] + pltpu.roll(second[9 * j + 8 : 9 * j + 9], PART, 1)
    row_avg = mine[18:19, 0:1] / FFW
    new_cols = 0.5 * cs_ref[...].reshape(1, D) + 0.5 * (wide[0:1, 0:D] / FFW + 1e-06)
    nc_ref[...] = new_cols.reshape(D)
    total_sq = row_avg * jnp.sum(wide[1:2, 0:D] / new_cols, axis=1, keepdims=True)
    rms = jnp.sqrt(total_sq / (FFW * D))
    factor = 0.1 / jnp.maximum(1.0, rms) * jnp.sqrt(row_avg)
    scaled = gwide[0:OWN, 0:D] * (lax.rsqrt(rows8[0:OWN]) * factor) * lax.rsqrt(new_cols)
    nw_ref[...] = (w_ref[...].astype(F32) - scaled).astype(jnp.bfloat16)

    for cp in core + started:
        cp.wait_send()


def per_device(tokens, grad_out, counts, weight, row_state, col_state):
    vmem = pl.BlockSpec(memory_space=pltpu.VMEM)
    smem = pl.BlockSpec(memory_space=pltpu.SMEM)
    dma = pltpu.SemaphoreType.DMA
    return pl.pallas_call(
        kernel,
        out_shape=(
            jax.ShapeDtypeStruct((OWN, D), jnp.bfloat16),
            jax.ShapeDtypeStruct((OWN,), F32),
            jax.ShapeDtypeStruct((D,), F32),
        ),
        in_specs=[vmem, vmem, smem, vmem, smem, vmem, vmem],
        out_specs=(vmem, vmem, vmem),
        scratch_shapes=[
            pltpu.VMEM((2, 256, HALF), jnp.bfloat16),
            pltpu.VMEM((NX, 96, 256), jnp.bfloat16),
            pltpu.VMEM((NX, 4, 24, HALF), F32),
            pltpu.VMEM((NX, 4, 24, HALF), F32),
            pltpu.VMEM((NX, 4, 24, HALF), F32),
            pltpu.VMEM((2, 2, 24, HALF), F32),
            pltpu.VMEM((2, 4, 24, HALF), F32),
            pltpu.VMEM((NZ, 16, HALF), F32),
            pltpu.VMEM((16, HALF), F32),
            pltpu.VMEM((16, HALF), F32),
            pltpu.VMEM((16, 128), F32),
            pltpu.VMEM((16, 128), F32),
            pltpu.VMEM((NY, 24, 128), F32),
            pltpu.VMEM((NZ, 24, 128), F32),
            pltpu.VMEM((NX, 24, 128), F32),
            pltpu.VMEM((24, 128), F32),
            pltpu.VMEM((24, 128), F32),
            pltpu.VMEM((8, 2 * WIDE + 128), F32),
            pltpu.VMEM((8, 2 * WIDE + 128), F32),
            dma((4,)), dma((4,)), dma((2, 2)), dma((2, 2)), dma((2, 4)), dma((2, 4)),
            dma((NZ,)), dma((NZ,)), dma((3,)), dma((3,)),
            dma((NY,)), dma((NY,)), dma((NZ,)), dma((NZ,)), dma((NX,)), dma((NX,)),
        ],
        compiler_params=pltpu.CompilerParams(
            collective_id=0, has_side_effects=True, vmem_limit_bytes=40 * 2**20
        ),
    )(tokens, grad_out, counts, weight, row_state, col_state, jnp.asarray(row_order(), jnp.bfloat16))


def solution(mesh):
    placed = (
        P("dp", None),
        P("dp", "expert"),
        P("dp"),
        P(("expert", "dp"), None),
        P(("expert", "dp")),
        P(),
    )
    return jax.shard_map(
        per_device,
        mesh=mesh,
        in_specs=placed,
        out_specs=(P(("expert", "dp"), None), P(("expert", "dp")), P()),
        check_vma=False,
    )
```

```python
import jax
import jax.numpy as jnp
import numpy as np
from jax import lax
from jax.experimental import pallas as pl
from jax.experimental.pallas import tpu as pltpu
from jax.sharding import PartitionSpec as P

D = 2080
FFW = 3072
NY, NZ, NX = 8, 8, 4
OWN = 6
ROWS = 12
WIDE = 1024
PART = 16
UNIT = (24, 512)
MESH = pl.DeviceIdType.MESH
F32 = jnp.float32
BF16 = jnp.bfloat16


def row_order():
    pick = np.zeros((2, NX, NZ, 24, 384), np.float32)
    tail = np.zeros((NZ, NX, 16, 384), np.float32)
    for x in range(NX):
        for z in range(NZ):
            for k in range(ROWS):
                unit = (z * NX + x) * ROWS + k
                pick[0, x, z, k, unit] = 1
                pick[1, x, z, ROWS + k, unit] = 1
                tail[z, x, k, unit] = 1
    return np.concatenate([pick.reshape(1536, 384), tail.reshape(512, 384)], axis=0)


def kernel(
    tok_ref, go_ref, cnt_ref, w_ref, rs_ref, cs_ref, pick_ref,
    nw_ref, nr_ref, nc_ref,
    lhs, lhs_t, rhs_t, other, acc, core_in, other_t, acc_t, core_t, d2_in, d1_in, z_in, xt_in, zt_in,
    mine_t, g_own, g_sib, gt_own, gt_sib, r_own, r_sib, st_a, st_b, st_f, wide, gwide,
    core_s, core_r, d2_s, d2_r, d1_s, d1_r, zs, zr, xts, xtr, zts, ztr, gs, gr,
    sas, sar, sbs, sbr, sfs, sfr,
):
    e = lax.axis_index("expert")
    q = lax.axis_index("dp")
    c, x, z = q % 2, (q // 2) % NX, q // (2 * NX)

    def at(ee, zz, xx, cc):
        return (ee, (zz * NX + xx) * 2 + cc)

    sib = at(e, z, x, 1 - c)
    y_peers = [at((e + d) % NY, z, x, c) for d in range(1, NY)]
    z_peers = [at(e, (z + d) % NZ, x, c) for d in range(1, NZ)]
    x_peers = [at(e, z, (x + d) % NX, c) for d in range(1, NX)]
    o_peers = [at(e, z, (x + d) % NX, 1 - c) for d in range(1, NX)]
    right, left = x_peers[0], x_peers[2]

    barrier = pltpu.get_barrier_semaphore()
    everyone = [sib] + y_peers + z_peers + x_peers + o_peers
    for peer in everyone:
        pl.semaphore_signal(barrier, inc=1, device_id=peer, device_id_type=MESH)

    def remote(src, dst, s, r, peer):
        return pltpu.make_async_remote_copy(
            src_ref=src, dst_ref=dst, send_sem=s, recv_sem=r, device_id=peer, device_id_type=MESH
        )

    started = []

    def send(*args):
        cp = remote(*args)
        cp.start()
        started.append(cp)
        return cp

    def arrived(buf, sem):
        remote(buf, buf, sem, sem, sib).wait_recv()

    def nt(a, b):
        return lax.dot_general(a, b, (((1,), (1,)), ((), ())), preferred_element_type=F32)

    live = lax.broadcasted_iota(jnp.int32, (256, 384), 0) < cnt_ref[0]
    masked = jnp.where(live, go_ref[...].astype(F32), 0.0).astype(BF16)
    lhs[...] = nt(pick_ref[0:1536, :], masked).astype(BF16).reshape(2, NX, 192, 256)
    picked_t = nt(pick_ref[1536:2048, :], masked).astype(BF16)
    rhs_t[...] = jnp.zeros_like(rhs_t)
    for k in range(NZ):
        lhs_t[:, 256 * k : 256 * (k + 1)] = picked_t[64 * k : 64 * (k + 1)]
        for h in range(2):
            rhs_t[h, PART * k : PART * (k + 1), 256 * k : 256 * (k + 1)] = tok_ref[
                2 * WIDE + PART * h : 2 * WIDE + PART * (h + 1), :
            ]

    def half(k, h):
        first = pl.multiple_of(WIDE * h, WIDE)
        out = nt(lhs[0, k], tok_ref[pl.ds(first, 512), :]) + nt(lhs[1, k], tok_ref[pl.ds(first + 512, 512), :])
        return out.reshape((NZ,) + UNIT)

    def product(k, _):
        other[k] = half(k, 1 - c)
        acc[k] = half(k, c)
        return 0

    lax.fori_loop(0, NX, product, 0)
    other_t[...] = nt(lhs_t[...], rhs_t[1 - c]).reshape(NX, 16, 128)
    acc_t[...] = nt(lhs_t[...], rhs_t[c]).reshape(NX, 16, 128)
    pl.semaphore_wait(barrier, len(everyone))

    slabs = [(x + 2) % NX, (x + 1) % NX, (x + 3) % NX, x]
    core = [send(other.at[k], core_in.at[k], core_s.at[j], core_r.at[j], sib) for j, k in enumerate(slabs)]
    core.append(send(other_t, core_t, core_s.at[4], core_r.at[4], sib))

    def settle(j):
        core[j].wait_recv()
        acc[slabs[j]] += core_in[slabs[j]]

    def zat(d):
        return (z + d) % NZ

    halfway = ((4, 5, 6, 7), (3, 2, 1, 0))
    peer_of = (right, left)

    def skip(side, i):
        k = zat(halfway[side][i])
        send(acc.at[slabs[0], k], d2_in.at[side, i], d2_s.at[side, i], d2_r.at[side, i], peer_of[side])

    def step(side, d):
        k = zat(d)
        if d in halfway[side]:
            i = halfway[side].index(d)
            arrived(d2_in.at[side, i], d2_r.at[side, i])
            acc[slabs[1 + side], k] += d2_in[side, i]
        send(acc.at[slabs[1 + side], k], d1_in.at[side, d], d1_s.at[side, d], d1_r.at[side, d], peer_of[side])

    def deliver(d):
        for side in range(2):
            arrived(d1_in.at[side, d], d1_r.at[side, d])
        acc[x, zat(d)] += d1_in[0, d] + d1_in[1, d]
        if d:
            send(acc.at[x, zat(d)], z_in.at[z], zs.at[d], zr.at[z], z_peers[d - 1])

    settle(0)
    skip(0, 0)
    skip(1, 0)
    skip(0, 1)
    skip(1, 1)
    settle(1)
    settle(2)
    step(0, 3)
    step(1, 4)
    skip(0, 2)
    skip(1, 2)
    settle(3)
    core[4].wait_recv()
    acc_t[...] += core_t[...]
    for d in range(1, NX):
        k = (x + d) % NX
        send(acc_t.at[k], xt_in.at[x], xts.at[d], xtr.at[x], x_peers[d - 1])
    step(0, 4)
    step(1, 3)
    step(0, 5)
    step(1, 2)
    skip(0, 3)
    skip(1, 3)
    step(0, 2)
    step(1, 5)
    deliver(4)
    deliver(3)
    step(0, 6)
    step(1, 1)
    step(0, 1)
    step(1, 6)
    xt = acc_t[x]
    for d in range(1, NX):
        k = (x + d) % NX
        arrived(xt_in.at[k], xtr.at[k])
        xt += xt_in[k]
    mine_t[...] = xt
    for d in range(1, NZ):
        send(mine_t, zt_in.at[z], zts.at[d], ztr.at[z], z_peers[d - 1])
    deliver(5)
    deliver(2)
    step(0, 7)
    step(1, 7)
    step(0, 0)
    step(1, 0)
    deliver(6)
    deliver(1)
    deliver(7)
    deliver(0)
    total = acc[x, z]
    total_t = mine_t[...]
    for d in (4, 5, 3, 6, 2, 7, 1):
        k = zat(d)
        arrived(zt_in.at[k], ztr.at[k])
        total_t += zt_in[k]
        arrived(z_in.at[k], zr.at[k])
        total += z_in[k]

    lane = lax.broadcasted_iota(jnp.int32, (16, 128), 1)
    row = lax.broadcasted_iota(jnp.int32, (16, 128), 0)
    tail = jnp.where((row < ROWS) & (lane // PART == z), total_t, 0.0)
    g_own[...] = total
    gt_own[...] = tail

    squared = total * total
    squared_t = tail * tail
    state = jnp.zeros((16, 128), F32)
    for k in range(OWN):
        state = jnp.where(row == c * OWN + k, rs_ref[k], state)
    sums = jnp.sum(squared, axis=1, keepdims=True)
    sums = sums[0:16] + jnp.concatenate([sums[12:24], sums[0:4]], axis=0) + jnp.sum(squared_t, axis=1, keepdims=True)
    r_own[...] = jnp.where(lane < 64, sums, state)
    r_copy = send(r_own, r_sib, gs.at[0], gr.at[0], sib)
    g_copy = send(g_own, g_sib, gs.at[1], gr.at[1], sib)
    gt_copy = send(gt_own, gt_sib, gs.at[2], gr.at[2], sib)

    row24 = lax.broadcasted_iota(jnp.int32, (24, 1), 0)

    def columns(values, k):
        for h in range(2):
            part = jnp.sum(jnp.where((row24 < ROWS) == (h == 0), values, 0.0), axis=0, keepdims=True)
            for j in range(4):
                st_a[ma, k + 4 * h + j : k + 4 * h + j + 1, :] = part[:, 128 * j : 128 * (j + 1)]

    ma = jnp.where(c == 0, e, z)
    mb = jnp.where(c == 0, z, e)
    columns(squared, 0)
    st_a[ma, 8:9, :] = jnp.sum(squared_t, axis=0, keepdims=True)
    r_copy.wait_recv()
    both = r_own[...] + r_sib[...]
    new_rows = 0.5 * both[:, 64:65] + 0.5 * (both[:, 0:1] / D + 1e-06)
    inverse = 1.0 / new_rows
    columns(squared * jnp.concatenate([inverse[0:12], inverse[0:12]], axis=0), 9)
    st_a[ma, 17:18, :] = jnp.sum(squared_t * inverse, axis=0, keepdims=True)
    row_part = jnp.sum(jnp.where(row[:, 0:1] < ROWS, new_rows, 0.0), axis=0, keepdims=True)
    st_a[ma, 18:24, :] = jnp.broadcast_to(row_part, (6, 128))

    def exchange(buf, me, s, r, peers):
        for d in range(1, 8):
            send(buf.at[me], buf.at[me], s.at[d], r.at[me], peers[d - 1])
        for d in (7, 1, 6, 2, 5, 3, 4):
            k = (me + d) % 8
            arrived(buf.at[k], r.at[k])
        out = buf[0]
        for k in range(1, 8):
            out += buf[k]
        return out

    def either(a, b):
        return tuple(jnp.where(c == 0, i, j) for i, j in zip(a, b))

    st_b[mb] = exchange(st_a, ma, sas, sar, [either(a, b) for a, b in zip(y_peers, z_peers)])
    st_f[c, x] = exchange(st_b, mb, sbs, sbr, [either(b, a) for a, b in zip(y_peers, z_peers)])
    send(st_f.at[c, x], st_f.at[c, x], sfs.at[6], sfr.at[c, x], sib)
    for d in range(1, NX):
        send(st_f.at[c, x], st_f.at[c, x], sfs.at[d - 1], sfr.at[c, x], x_peers[d - 1])
        send(st_f.at[c, x], st_f.at[c, x], sfs.at[d + 2], sfr.at[c, x], o_peers[d - 1])

    def halves(own, sibling):
        return jnp.where(c == 0, own, sibling), jnp.where(c == 0, sibling, own)

    def fold(v):
        for shift in (64, 32, 16):
            v = v + pltpu.roll(v, shift, 1)
        return v

    def rows_of(v, first):
        return jnp.where(c == 0, v[first : first + 6], v[first + 6 : first + 12])

    g_copy.wait_recv()
    gt_copy.wait_recv()
    low, high = halves(g_own[...], g_sib[...])
    for h in range(2):
        gwide[0:OWN, 512 * h : 512 * (h + 1)] = rows_of(low, ROWS * h)
        gwide[0:OWN, WIDE + 512 * h : WIDE + 512 * (h + 1)] = rows_of(high, ROWS * h)
    low, high = halves(fold(gt_own[...]), fold(gt_sib[...]))
    gwide[0:OWN, 2 * WIDE :] = rows_of(jnp.where(lane < PART, low, high), 0)
    rows6 = rows_of(new_rows, 0)
    eye = lax.broadcasted_iota(jnp.int32, (OWN, 128), 0) == lax.broadcasted_iota(jnp.int32, (OWN, 128), 1)
    nr_ref[...] = jnp.sum(jnp.where(eye, rows6, 0.0), axis=0)[0:OWN]

    arrived(st_f.at[1 - c, x], sfr.at[1 - c, x])
    for d in range(1, NX):
        for cc in range(2):
            k = (x + d) % NX
            core_k = (c + cc) % 2
            arrived(st_f.at[core_k, k], sfr.at[core_k, k])
    sums = []
    for cc in range(2):
        v = st_f[cc, 0]
        for k in range(1, NX):
            v += st_f[cc, k]
        sums.append(v)
    for cc in range(2):
        for j in range(2):
            for k in range(8):
                first = WIDE * cc + 128 * k
                wide[j : j + 1, first : first + 128] = sums[cc][9 * j + k : 9 * j + k + 1]
    for j in range(2):
        low, high = (fold(v[9 * j + 8 : 9 * j + 9]) for v in sums)
        wide[j : j + 1, 2 * WIDE :] = jnp.where(lane[0:1] < PART, low, high)
    row_avg = sums[0][18:19, 0:1] / FFW
    new_cols = 0.5 * cs_ref[...].reshape(1, D) + 0.5 * (wide[0:1, 0:D] / FFW + 1e-06)
    nc_ref[...] = new_cols.reshape(D)
    total_sq = row_avg * jnp.sum(wide[1:2, 0:D] / new_cols, axis=1, keepdims=True)
    rms = jnp.sqrt(total_sq / (FFW * D))
    factor = 0.1 / jnp.maximum(1.0, rms) * jnp.sqrt(row_avg)
    scaled = gwide[0:OWN, 0:D] * (lax.rsqrt(rows6) * factor) * lax.rsqrt(new_cols)
    nw_ref[...] = (w_ref[...].astype(F32) - scaled).astype(BF16)

    for cp in started:
        cp.wait_send()


def per_device(tokens, grad_out, counts, weight, row_state, col_state):
    vmem = pl.BlockSpec(memory_space=pltpu.VMEM)
    smem = pl.BlockSpec(memory_space=pltpu.SMEM)
    dma = pltpu.SemaphoreType.DMA

    def f32(*shape):
        return pltpu.VMEM(shape, F32)

    return pl.pallas_call(
        kernel,
        out_shape=(
            jax.ShapeDtypeStruct((OWN, D), BF16),
            jax.ShapeDtypeStruct((OWN,), F32),
            jax.ShapeDtypeStruct((D,), F32),
        ),
        in_specs=[vmem, vmem, smem, vmem, smem, vmem, vmem],
        out_specs=(vmem, vmem, vmem),
        scratch_shapes=[
            pltpu.VMEM((2, NX, 192, 256), BF16),
            pltpu.VMEM((64, 2048), BF16),
            pltpu.VMEM((2, 128, 2048), BF16),
            f32(NX, NZ, *UNIT), f32(NX, NZ, *UNIT), f32(NX, NZ, *UNIT),
            f32(NX, 16, 128), f32(NX, 16, 128), f32(NX, 16, 128),
            f32(2, 4, *UNIT), f32(2, NZ, *UNIT), f32(NZ, *UNIT),
            f32(NX, 16, 128), f32(NZ, 16, 128), f32(16, 128),
            f32(*UNIT), f32(*UNIT), f32(16, 128), f32(16, 128), f32(16, 128), f32(16, 128),
            f32(8, 24, 128), f32(8, 24, 128), f32(2, NX, 24, 128),
            f32(8, 2 * WIDE + 128), f32(8, 2 * WIDE + 128),
            dma((5,)), dma((5,)), dma((2, 4)), dma((2, 4)), dma((2, NZ)), dma((2, NZ)),
            dma((NZ,)), dma((NZ,)), dma((NX,)), dma((NX,)), dma((NZ,)), dma((NZ,)), dma((3,)), dma((3,)),
            dma((8,)), dma((8,)), dma((8,)), dma((8,)), dma((7,)), dma((2, NX)),
        ],
        compiler_params=pltpu.CompilerParams(
            collective_id=0, has_side_effects=True, vmem_limit_bytes=40 * 2**20
        ),
    )(tokens.T, grad_out, counts, weight, row_state, col_state, jnp.asarray(row_order(), BF16))


def solution(mesh):
    placed = (
        P("dp", None),
        P("dp", "expert"),
        P("dp"),
        P(("expert", "dp"), None),
        P(("expert", "dp")),
        P(),
    )
    return jax.shard_map(
        per_device,
        mesh=mesh,
        in_specs=placed,
        out_specs=(P(("expert", "dp"), None), P(("expert", "dp")), P()),
        check_vma=False,
    )
```

```python
import jax
import jax.numpy as jnp
from jax import lax
from jax.experimental import pallas as pl
from jax.experimental.pallas import tpu as pltpu
from jax.sharding import PartitionSpec as P

D = 2080
FFW = 3072
NY, NZ, NX = 8, 8, 4
OWN = 6
ROWS = 12
WIDE = 1024
PART = 16
UNIT = (24, 512)
MESH = pl.DeviceIdType.MESH
F32 = jnp.float32
BF16 = jnp.bfloat16


def kernel(
    tok_hbm, go_hbm, cnt_hbm, w_hbm, rs_hbm, cs_hbm,
    nw_ref, nr_ref, nc_ref,
    tok_ref, go_ref, cnt_ref, w_ref, rs_ref, cs_ref, in_s, lhs, picked_t, lhs_t, rhs_t, other, acc, core_in, other_t, acc_t, core_t, d2_in, d1_in, z_in, xt_in, zt_in,
    mine_t, g_own, g_sib, gt_own, gt_sib, r_own, r_sib, st_a, st_b, st_f, wide, gwide,
    first_s, first_r, core_s, core_r, d2_s, d2_r, d1_s, d1_r, zs, zr, xts, xtr, zts, ztr, gs, gr,
    sas, sar, sbs, sbr, sfs, sfr,
):
    e = lax.axis_index("expert")
    q = lax.axis_index("dp")
    c, x, z = q % 2, (q // 2) % NX, q // (2 * NX)

    def at(ee, zz, xx, cc):
        return (ee, (zz * NX + xx) * 2 + cc)

    sib = at(e, z, x, 1 - c)
    y_peers = [at((e + d) % NY, z, x, c) for d in range(1, NY)]
    z_peers = [at(e, (z + d) % NZ, x, c) for d in range(1, NZ)]
    x_peers = [at(e, z, (x + d) % NX, c) for d in range(1, NX)]
    o_peers = [at(e, z, (x + d) % NX, 1 - c) for d in range(1, NX)]
    right, left = x_peers[0], x_peers[2]

    loads = [
        pltpu.make_async_copy(src, dst, in_s.at[k])
        for k, (src, dst) in enumerate(
            [(cnt_hbm, cnt_ref), (go_hbm, go_ref), (tok_hbm, tok_ref), (rs_hbm, rs_ref), (cs_hbm, cs_ref), (w_hbm, w_ref)]
        )
    ]
    for cp in loads:
        cp.start()
    barrier = pltpu.get_barrier_semaphore()
    everyone = [sib] + y_peers + z_peers + x_peers + o_peers
    for peer in everyone:
        pl.semaphore_signal(barrier, inc=1, device_id=peer, device_id_type=MESH)

    def remote(src, dst, s, r, peer):
        return pltpu.make_async_remote_copy(
            src_ref=src, dst_ref=dst, send_sem=s, recv_sem=r, device_id=peer, device_id_type=MESH
        )

    started = []

    def send(*args):
        cp = remote(*args)
        cp.start()
        started.append(cp)
        return cp

    def arrived(buf, sem):
        remote(buf, buf, sem, sem, sib).wait_recv()

    def nt(a, b):
        return lax.dot_general(a, b, (((1,), (1,)), ((), ())), preferred_element_type=F32)

    row = lax.broadcasted_iota(jnp.int32, (512, 384), 0)
    k = row & 15
    unit = ((row >> 4) & 7) * (NX * ROWS) + (row >> 7) * ROWS + k
    pick = (lax.broadcasted_iota(jnp.int32, (512, 384), 1) == unit) & (k < ROWS)
    pick = jnp.where(pick, 1.0, 0.0).astype(BF16)
    loads[0].wait()
    loads[1].wait()
    live = lax.broadcasted_iota(jnp.int32, (256, 384), 0) < cnt_ref[0]
    masked = jnp.where(live, go_ref[...].astype(F32), 0.0).astype(BF16)
    picked = nt(pick, masked)
    picked_t[...] = picked.astype(BF16).reshape(NX, 128, 256)
    units = picked.reshape(NX * NZ, 16, 256)
    blank = jnp.zeros((NX * NZ, 8, 256), F32)
    lhs[0] = jnp.concatenate([units, blank], axis=1).reshape(768, 256).astype(BF16).reshape(NX, 192, 256)
    moved = jnp.concatenate([blank, pltpu.roll(units, 4, 1)], axis=1)
    lhs[1] = moved.reshape(768, 256).astype(BF16).reshape(NX, 192, 256)

    def half(k, h):
        first = pl.multiple_of(WIDE * h, WIDE)
        out = nt(lhs[0, k], tok_ref[pl.ds(first, 512), :]) + nt(lhs[1, k], tok_ref[pl.ds(first + 512, 512), :])
        return out.reshape((NZ,) + UNIT)

    loads[2].wait()
    slabs = [(x + 2) % NX, (x + 1) % NX, (x + 3) % NX, x]

    def zat(d):
        return (z + d) % NZ

    def offer(j):
        k = slabs[j]
        other[k] = half(k, 1 - c)
        send(other.at[k], core_in.at[k], core_s.at[j], core_r.at[j], sib)

    def settle(j):
        k = slabs[j]
        arrived(core_in.at[k], core_r.at[j])
        acc[k] += core_in[k]

    def own(j):
        acc[slabs[j]] = half(slabs[j], c)

    halfway = ((4, 5, 6, 7), (3, 2, 1, 0))
    peer_of = (right, left)

    def skip(side, i):
        k = zat(halfway[side][i])
        arrived(core_in.at[slabs[0], k], first_r.at[4 * side + i])
        acc[slabs[0], k] += core_in[slabs[0], k]
        send(acc.at[slabs[0], k], d2_in.at[side, i], d2_s.at[side, i], d2_r.at[side, i], peer_of[side])

    def step(side, d):
        k = zat(d)
        if d in halfway[side]:
            i = halfway[side].index(d)
            arrived(d2_in.at[side, i], d2_r.at[side, i])
            acc[slabs[1 + side], k] += d2_in[side, i]
        send(acc.at[slabs[1 + side], k], d1_in.at[side, d], d1_s.at[side, d], d1_r.at[side, d], peer_of[side])

    def deliver(d):
        for side in range(2):
            arrived(d1_in.at[side, d], d1_r.at[side, d])
        acc[x, zat(d)] += d1_in[0, d] + d1_in[1, d]
        if d:
            send(acc.at[x, zat(d)], z_in.at[z], zs.at[d], zr.at[z], z_peers[d - 1])

    other[slabs[0]] = half(slabs[0], 1 - c)
    pl.semaphore_wait(barrier, len(everyone))
    for i in range(4):
        for side in range(2):
            k, j = zat(halfway[side][i]), 4 * side + i
            send(other.at[slabs[0], k], core_in.at[slabs[0], k], first_s.at[j], first_r.at[j], sib)
    own(0)
    for i in range(3):
        skip(0, i)
        skip(1, i)
    offer(1)
    offer(2)
    own(1)
    settle(1)
    step(0, 3)
    own(2)
    settle(2)
    step(1, 4)
    step(0, 4)
    step(1, 3)
    offer(3)
    rhs_t[...] = jnp.zeros_like(rhs_t)
    for k in range(NZ):
        for j in range(NX):
            lhs_t[16 * j : 16 * (j + 1), 256 * k : 256 * (k + 1)] = picked_t[j, 16 * k : 16 * (k + 1), :]
        for h in range(2):
            rhs_t[h, PART * k : PART * (k + 1), 256 * k : 256 * (k + 1)] = tok_ref[
                2 * WIDE + PART * h : 2 * WIDE + PART * (h + 1), :
            ]
    other_t[...] = nt(lhs_t[...], rhs_t[1 - c]).reshape(NX, 16, 128)
    send(other_t, core_t, core_s.at[0], core_r.at[0], sib)
    acc_t[...] = nt(lhs_t[...], rhs_t[c]).reshape(NX, 16, 128)
    own(3)
    settle(3)
    step(0, 5)
    step(1, 2)
    arrived(core_t, core_r.at[0])
    acc_t[...] += core_t[...]
    for d in range(1, NX):
        k = (x + d) % NX
        send(acc_t.at[k], xt_in.at[x], xts.at[d], xtr.at[x], x_peers[d - 1])
    skip(0, 3)
    skip(1, 3)
    step(0, 2)
    step(1, 5)
    deliver(4)
    deliver(3)
    step(0, 6)
    step(1, 1)
    step(0, 1)
    step(1, 6)
    xt = acc_t[x]
    for d in range(1, NX):
        k = (x + d) % NX
        arrived(xt_in.at[k], xtr.at[k])
        xt += xt_in[k]
    mine_t[...] = xt
    for d in range(1, NZ):
        send(mine_t, zt_in.at[z], zts.at[d], ztr.at[z], z_peers[d - 1])
    deliver(5)
    deliver(2)
    step(0, 7)
    step(1, 7)
    step(0, 0)
    step(1, 0)
    deliver(6)
    deliver(1)
    deliver(7)
    deliver(0)
    total = acc[x, z]
    total_t = mine_t[...]
    for d in (4, 5, 3, 6, 2, 7, 1):
        k = zat(d)
        arrived(zt_in.at[k], ztr.at[k])
        total_t += zt_in[k]
        arrived(z_in.at[k], zr.at[k])
        total += z_in[k]

    lane = lax.broadcasted_iota(jnp.int32, (16, 128), 1)
    row = lax.broadcasted_iota(jnp.int32, (16, 128), 0)
    tail = jnp.where((row < ROWS) & (lane // PART == z), total_t, 0.0)
    g_own[...] = total
    gt_own[...] = tail

    for cp in loads[3:]:
        cp.wait()
    squared = total * total
    squared_t = tail * tail
    state = jnp.zeros((16, 128), F32)
    for k in range(OWN):
        state = jnp.where(row == c * OWN + k, rs_ref[k], state)
    sums = jnp.sum(squared, axis=1, keepdims=True)
    sums = sums[0:16] + jnp.concatenate([sums[12:24], sums[0:4]], axis=0) + jnp.sum(squared_t, axis=1, keepdims=True)
    r_own[...] = jnp.where(lane < 64, sums, state)
    r_copy = send(r_own, r_sib, gs.at[0], gr.at[0], sib)
    g_copy = send(g_own, g_sib, gs.at[1], gr.at[1], sib)
    gt_copy = send(gt_own, gt_sib, gs.at[2], gr.at[2], sib)

    row24 = lax.broadcasted_iota(jnp.int32, (24, 1), 0)

    def columns(values, k):
        for h in range(2):
            part = jnp.sum(jnp.where((row24 < ROWS) == (h == 0), values, 0.0), axis=0, keepdims=True)
            for j in range(4):
                st_a[ma, k + 4 * h + j : k + 4 * h + j + 1, :] = part[:, 128 * j : 128 * (j + 1)]

    ma = jnp.where(c == 0, e, z)
    mb = jnp.where(c == 0, z, e)
    columns(squared, 0)
    st_a[ma, 8:9, :] = jnp.sum(squared_t, axis=0, keepdims=True)
    r_copy.wait_recv()
    both = r_own[...] + r_sib[...]
    new_rows = 0.5 * both[:, 64:65] + 0.5 * (both[:, 0:1] / D + 1e-06)
    inverse = 1.0 / new_rows
    columns(squared * jnp.concatenate([inverse[0:12], inverse[0:12]], axis=0), 9)
    st_a[ma, 17:18, :] = jnp.sum(squared_t * inverse, axis=0, keepdims=True)
    row_part = jnp.sum(jnp.where(row[:, 0:1] < ROWS, new_rows, 0.0), axis=0, keepdims=True)
    st_a[ma, 18:24, :] = jnp.broadcast_to(row_part, (6, 128))

    def exchange(buf, me, s, r, peers):
        for d in range(1, 8):
            send(buf.at[me], buf.at[me], s.at[d], r.at[me], peers[d - 1])
        for d in (7, 1, 6, 2, 5, 3, 4):
            k = (me + d) % 8
            arrived(buf.at[k], r.at[k])
        out = buf[0]
        for k in range(1, 8):
            out += buf[k]
        return out

    def either(a, b):
        return tuple(jnp.where(c == 0, i, j) for i, j in zip(a, b))

    st_b[mb] = exchange(st_a, ma, sas, sar, [either(a, b) for a, b in zip(y_peers, z_peers)])
    st_f[c, x] = exchange(st_b, mb, sbs, sbr, [either(b, a) for a, b in zip(y_peers, z_peers)])
    send(st_f.at[c, x], st_f.at[c, x], sfs.at[6], sfr.at[c, x], sib)
    for d in range(1, NX):
        send(st_f.at[c, x], st_f.at[c, x], sfs.at[d - 1], sfr.at[c, x], x_peers[d - 1])
        send(st_f.at[c, x], st_f.at[c, x], sfs.at[d + 2], sfr.at[c, x], o_peers[d - 1])

    def halves(own, sibling):
        return jnp.where(c == 0, own, sibling), jnp.where(c == 0, sibling, own)

    def fold(v):
        for shift in (64, 32, 16):
            v = v + pltpu.roll(v, shift, 1)
        return v

    def rows_of(v, first):
        return jnp.where(c == 0, v[first : first + 6], v[first + 6 : first + 12])

    g_copy.wait_recv()
    gt_copy.wait_recv()
    low, high = halves(g_own[...], g_sib[...])
    for h in range(2):
        gwide[0:OWN, 512 * h : 512 * (h + 1)] = rows_of(low, ROWS * h)
        gwide[0:OWN, WIDE + 512 * h : WIDE + 512 * (h + 1)] = rows_of(high, ROWS * h)
    low, high = halves(fold(gt_own[...]), fold(gt_sib[...]))
    gwide[0:OWN, 2 * WIDE :] = rows_of(jnp.where(lane < PART, low, high), 0)
    rows6 = rows_of(new_rows, 0)
    eye = lax.broadcasted_iota(jnp.int32, (OWN, 128), 0) == lax.broadcasted_iota(jnp.int32, (OWN, 128), 1)
    nr_ref[...] = jnp.sum(jnp.where(eye, rows6, 0.0), axis=0)[0:OWN]

    arrived(st_f.at[1 - c, x], sfr.at[1 - c, x])
    for d in range(1, NX):
        for cc in range(2):
            k = (x + d) % NX
            core_k = (c + cc) % 2
            arrived(st_f.at[core_k, k], sfr.at[core_k, k])
    sums = []
    for cc in range(2):
        v = st_f[cc, 0]
        for k in range(1, NX):
            v += st_f[cc, k]
        sums.append(v)
    for cc in range(2):
        for j in range(2):
            for k in range(8):
                first = WIDE * cc + 128 * k
                wide[j : j + 1, first : first + 128] = sums[cc][9 * j + k : 9 * j + k + 1]
    for j in range(2):
        low, high = (fold(v[9 * j + 8 : 9 * j + 9]) for v in sums)
        wide[j : j + 1, 2 * WIDE :] = jnp.where(lane[0:1] < PART, low, high)
    row_avg = sums[0][18:19, 0:1] / FFW
    new_cols = 0.5 * cs_ref[...].reshape(1, D) + 0.5 * (wide[0:1, 0:D] / FFW + 1e-06)
    nc_ref[...] = new_cols.reshape(D)
    total_sq = row_avg * jnp.sum(wide[1:2, 0:D] / new_cols, axis=1, keepdims=True)
    rms = jnp.sqrt(total_sq / (FFW * D))
    factor = 0.1 / jnp.maximum(1.0, rms) * jnp.sqrt(row_avg)
    scaled = gwide[0:OWN, 0:D] * (lax.rsqrt(rows6) * factor) * lax.rsqrt(new_cols)
    nw_ref[...] = (w_ref[...].astype(F32) - scaled).astype(BF16)

    for cp in started:
        cp.wait_send()


def store(a, b, c, a_out, b_out, c_out, sem):
    copies = [pltpu.make_async_copy(src, dst, sem.at[k]) for k, (src, dst) in enumerate([(a, a_out), (b, b_out), (c, c_out)])]
    for cp in copies:
        cp.start()
    for cp in copies:
        cp.wait()


def per_device(tokens, grad_out, counts, weight, row_state, col_state):
    vmem = pl.BlockSpec(memory_space=pltpu.VMEM)
    dma = pltpu.SemaphoreType.DMA

    def f32(*shape):
        return pltpu.VMEM(shape, F32)

    hbm = pl.BlockSpec(memory_space=pltpu.MemorySpace.HBM)
    results = (
        jax.ShapeDtypeStruct((OWN, D), BF16),
        jax.ShapeDtypeStruct((OWN,), F32),
        jax.ShapeDtypeStruct((D,), F32),
    )
    computed = pl.pallas_call(
        kernel,
        out_shape=tuple(pltpu.VMEM(r.shape, r.dtype) for r in results),
        in_specs=[hbm] * 6,
        out_specs=(vmem, vmem, vmem),
        scratch_shapes=[
            pltpu.VMEM((D, 256), BF16), pltpu.VMEM((256, 384), BF16), pltpu.SMEM((1,), jnp.int32),
            pltpu.VMEM((OWN, D), BF16), pltpu.SMEM((OWN,), F32), pltpu.VMEM((D,), F32), dma((6,)),
            pltpu.VMEM((2, NX, 192, 256), BF16),
            pltpu.VMEM((NX, 128, 256), BF16),
            pltpu.VMEM((64, 2048), BF16),
            pltpu.VMEM((2, 128, 2048), BF16),
            f32(NX, NZ, *UNIT), f32(NX, NZ, *UNIT), f32(NX, NZ, *UNIT),
            f32(NX, 16, 128), f32(NX, 16, 128), f32(NX, 16, 128),
            f32(2, 4, *UNIT), f32(2, NZ, *UNIT), f32(NZ, *UNIT),
            f32(NX, 16, 128), f32(NZ, 16, 128), f32(16, 128),
            f32(*UNIT), f32(*UNIT), f32(16, 128), f32(16, 128), f32(16, 128), f32(16, 128),
            f32(8, 24, 128), f32(8, 24, 128), f32(2, NX, 24, 128),
            f32(8, 2 * WIDE + 128), f32(8, 2 * WIDE + 128),
            dma((8,)), dma((8,)), dma((4,)), dma((4,)), dma((2, 4)), dma((2, 4)), dma((2, NZ)), dma((2, NZ)),
            dma((NZ,)), dma((NZ,)), dma((NX,)), dma((NX,)), dma((NZ,)), dma((NZ,)), dma((3,)), dma((3,)),
            dma((8,)), dma((8,)), dma((8,)), dma((8,)), dma((7,)), dma((2, NX)),
        ],
        compiler_params=pltpu.CompilerParams(
            collective_id=0, has_side_effects=True, vmem_limit_bytes=56 * 2**20
        ),
    )(tokens.T, grad_out, counts, weight, row_state, col_state)
    return pl.pallas_call(
        store,
        out_shape=results,
        in_specs=[vmem] * 3,
        out_specs=(hbm, hbm, hbm),
        scratch_shapes=[dma((3,))],
    )(*computed)


def solution(mesh):
    placed = (
        P("dp", None),
        P("dp", "expert"),
        P("dp"),
        P(("expert", "dp"), None),
        P(("expert", "dp")),
        P(),
    )
    return jax.shard_map(
        per_device,
        mesh=mesh,
        in_specs=placed,
        out_specs=(P(("expert", "dp"), None), P(("expert", "dp")), P()),
        check_vma=False,
    )
```

```python
import jax
import jax.numpy as jnp
from jax import lax
from jax.experimental import pallas as pl
from jax.experimental.pallas import tpu as pltpu
from jax.sharding import PartitionSpec as P

D = 2080
FFW = 3072
NY, NZ, NX = 8, 8, 4
OWN = 6
ROWS = 12
WIDE = 1024
PART = 16
UNIT = (24, 512)
MESH = pl.DeviceIdType.MESH
F32 = jnp.float32
BF16 = jnp.bfloat16


def kernel(
    tok_hbm, go_hbm, cnt_hbm, w_hbm, rs_hbm, cs_hbm,
    nw_ref, nr_ref, nc_ref,
    tok_ref, go_ref, cnt_ref, w_ref, rs_ref, cs_ref, in_s, lhs, picked_t, lhs_t, rhs_t, other, acc, core_in, other_t, acc_t, core_t, d2_in, d1_in, z_in, xt_in, zt_in,
    mine_t, g_own, g_sib, gt_own, gt_sib, r_own, r_sib, st_a, st_b, st_f, wide, gwide,
    first_s, first_r, core_s, core_r, d2_s, d2_r, d1_s, d1_r, zs, zr, xts, xtr, zts, ztr, gs, gr,
    sas, sar, sbs, sbr, sfs, sfr,
):
    e = lax.axis_index("expert")
    q = lax.axis_index("dp")
    c, x, z = q % 2, (q // 2) % NX, q // (2 * NX)

    def at(ee, zz, xx, cc):
        return (ee, (zz * NX + xx) * 2 + cc)

    sib = at(e, z, x, 1 - c)
    y_peers = [at((e + d) % NY, z, x, c) for d in range(1, NY)]
    z_peers = [at(e, (z + d) % NZ, x, c) for d in range(1, NZ)]
    x_peers = [at(e, z, (x + d) % NX, c) for d in range(1, NX)]
    o_peers = [at(e, z, (x + d) % NX, 1 - c) for d in range(1, NX)]
    right, left = x_peers[0], x_peers[2]

    loads = [
        pltpu.make_async_copy(src, dst, in_s.at[k])
        for k, (src, dst) in enumerate(
            [(cnt_hbm, cnt_ref), (go_hbm, go_ref), (tok_hbm, tok_ref), (rs_hbm, rs_ref), (cs_hbm, cs_ref), (w_hbm, w_ref)]
        )
    ]
    for cp in loads:
        cp.start()
    barrier = pltpu.get_barrier_semaphore()
    everyone = [sib] + y_peers + z_peers + x_peers + o_peers
    for peer in everyone:
        pl.semaphore_signal(barrier, inc=1, device_id=peer, device_id_type=MESH)

    def remote(src, dst, s, r, peer):
        return pltpu.make_async_remote_copy(
            src_ref=src, dst_ref=dst, send_sem=s, recv_sem=r, device_id=peer, device_id_type=MESH
        )

    started = []

    def send(*args):
        cp = remote(*args)
        cp.start()
        started.append(cp)
        return cp

    def arrived(buf, sem):
        remote(buf, buf, sem, sem, sib).wait_recv()

    def nt(a, b):
        return lax.dot_general(a, b, (((1,), (1,)), ((), ())), preferred_element_type=F32)

    row = lax.broadcasted_iota(jnp.int32, (512, 384), 0)
    k = row & 15
    unit = ((row >> 4) & 7) * (NX * ROWS) + (row >> 7) * ROWS + k
    pick = (lax.broadcasted_iota(jnp.int32, (512, 384), 1) == unit) & (k < ROWS)
    pick = jnp.where(pick, 1.0, 0.0).astype(BF16)
    loads[0].wait()
    loads[1].wait()
    live = lax.broadcasted_iota(jnp.int32, (256, 384), 0) < cnt_ref[0]
    masked = jnp.where(live, go_ref[...].astype(F32), 0.0).astype(BF16)
    picked = nt(pick, masked)
    picked_t[...] = picked.astype(BF16).reshape(NX, 128, 256)
    units = picked.reshape(NX * NZ, 16, 256)
    blank = jnp.zeros((NX * NZ, 8, 256), F32)
    lhs[0] = jnp.concatenate([units, blank], axis=1).reshape(768, 256).astype(BF16).reshape(NX, 192, 256)
    moved = jnp.concatenate([blank, pltpu.roll(units, 4, 1)], axis=1)
    lhs[1] = moved.reshape(768, 256).astype(BF16).reshape(NX, 192, 256)

    def half(k, h):
        first = pl.multiple_of(WIDE * h, WIDE)
        out = nt(lhs[0, k], tok_ref[pl.ds(first, 512), :]) + nt(lhs[1, k], tok_ref[pl.ds(first + 512, 512), :])
        return out.reshape((NZ,) + UNIT)

    loads[2].wait()
    slabs = [(x + 2) % NX, (x + 1) % NX, (x + 3) % NX, x]

    def zat(d):
        return (z + d) % NZ

    def offer(j):
        k = slabs[j]
        other[k] = half(k, 1 - c)
        send(other.at[k], core_in.at[k], core_s.at[j], core_r.at[j], sib)

    def settle(j):
        k = slabs[j]
        arrived(core_in.at[k], core_r.at[j])
        acc[k] += core_in[k]

    def own(j):
        acc[slabs[j]] = half(slabs[j], c)

    halfway = ((4, 5, 6, 7), (3, 2, 1, 0))
    peer_of = (right, left)

    def skip(side, i):
        k = zat(halfway[side][i])
        arrived(core_in.at[slabs[0], k], first_r.at[4 * side + i])
        acc[slabs[0], k] += core_in[slabs[0], k]
        send(acc.at[slabs[0], k], d2_in.at[side, i], d2_s.at[side, i], d2_r.at[side, i], peer_of[side])

    def step(side, d):
        k = zat(d)
        if d in halfway[side]:
            i = halfway[side].index(d)
            arrived(d2_in.at[side, i], d2_r.at[side, i])
            acc[slabs[1 + side], k] += d2_in[side, i]
        send(acc.at[slabs[1 + side], k], d1_in.at[side, d], d1_s.at[side, d], d1_r.at[side, d], peer_of[side])

    def deliver(d):
        for side in range(2):
            arrived(d1_in.at[side, d], d1_r.at[side, d])
        acc[x, zat(d)] += d1_in[0, d] + d1_in[1, d]
        if d:
            send(acc.at[x, zat(d)], z_in.at[z], zs.at[d], zr.at[z], z_peers[d - 1])

    other[slabs[0]] = half(slabs[0], 1 - c)
    pl.semaphore_wait(barrier, len(everyone))
    for i in range(4):
        for side in range(2):
            k, j = zat(halfway[side][i]), 4 * side + i
            send(other.at[slabs[0], k], core_in.at[slabs[0], k], first_s.at[j], first_r.at[j], sib)
    own(0)
    for i in range(3):
        skip(0, i)
        skip(1, i)
    offer(1)
    offer(2)
    own(1)
    settle(1)
    step(0, 3)
    own(2)
    settle(2)
    step(1, 4)
    step(0, 4)
    step(1, 3)
    offer(3)
    rhs_t[...] = jnp.zeros_like(rhs_t)
    for k in range(NZ):
        for j in range(NX):
            lhs_t[16 * j : 16 * (j + 1), 256 * k : 256 * (k + 1)] = picked_t[j, 16 * k : 16 * (k + 1), :]
        for h in range(2):
            rhs_t[h, PART * k : PART * (k + 1), 256 * k : 256 * (k + 1)] = tok_ref[
                2 * WIDE + PART * h : 2 * WIDE + PART * (h + 1), :
            ]
    other_t[...] = nt(lhs_t[...], rhs_t[1 - c]).reshape(NX, 16, 128)
    send(other_t, core_t, core_s.at[0], core_r.at[0], sib)
    acc_t[...] = nt(lhs_t[...], rhs_t[c]).reshape(NX, 16, 128)
    own(3)
    settle(3)
    step(0, 5)
    step(1, 2)
    arrived(core_t, core_r.at[0])
    acc_t[...] += core_t[...]
    for d in range(1, NX):
        k = (x + d) % NX
        send(acc_t.at[k], xt_in.at[x], xts.at[d], xtr.at[x], x_peers[d - 1])
    skip(0, 3)
    skip(1, 3)
    step(0, 2)
    step(1, 5)
    deliver(4)
    deliver(3)
    step(0, 6)
    step(1, 1)
    step(0, 1)
    step(1, 6)
    xt = acc_t[x]
    for d in range(1, NX):
        k = (x + d) % NX
        arrived(xt_in.at[k], xtr.at[k])
        xt += xt_in[k]
    mine_t[...] = xt
    for d in range(1, NZ):
        send(mine_t, zt_in.at[z], zts.at[d], ztr.at[z], z_peers[d - 1])
    deliver(5)
    deliver(2)
    step(0, 7)
    step(1, 7)
    step(0, 0)
    step(1, 0)
    deliver(6)
    deliver(1)
    deliver(7)
    deliver(0)
    total = acc[x, z]
    total_t = mine_t[...]
    for d in (4, 5, 3, 6, 2, 7, 1):
        k = zat(d)
        arrived(zt_in.at[k], ztr.at[k])
        total_t += zt_in[k]
        arrived(z_in.at[k], zr.at[k])
        total += z_in[k]

    lane = lax.broadcasted_iota(jnp.int32, (16, 128), 1)
    row = lax.broadcasted_iota(jnp.int32, (16, 128), 0)
    tail = jnp.where((row < ROWS) & (lane // PART == z), total_t, 0.0)
    g_own[...] = total
    gt_own[...] = tail

    for cp in loads[3:]:
        cp.wait()
    squared = total * total
    squared_t = tail * tail
    state = jnp.zeros((16, 128), F32)
    for k in range(OWN):
        state = jnp.where(row == c * OWN + k, rs_ref[k], state)
    sums = jnp.sum(squared, axis=1, keepdims=True)
    sums = sums[0:16] + jnp.concatenate([sums[12:24], sums[0:4]], axis=0) + jnp.sum(squared_t, axis=1, keepdims=True)
    r_own[...] = jnp.where(lane < 64, sums, state)
    r_copy = send(r_own, r_sib, gs.at[0], gr.at[0], sib)
    g_copy = send(g_own, g_sib, gs.at[1], gr.at[1], sib)
    gt_copy = send(gt_own, gt_sib, gs.at[2], gr.at[2], sib)

    row24 = lax.broadcasted_iota(jnp.int32, (24, 1), 0)

    def columns(values, k):
        for h in range(2):
            part = jnp.sum(jnp.where((row24 < ROWS) == (h == 0), values, 0.0), axis=0, keepdims=True)
            for j in range(4):
                st_a[ma, k + 4 * h + j : k + 4 * h + j + 1, :] = part[:, 128 * j : 128 * (j + 1)]

    ma = jnp.where(c == 0, e, z)
    mb = jnp.where(c == 0, z, e)
    columns(squared, 0)
    st_a[ma, 8:9, :] = jnp.sum(squared_t, axis=0, keepdims=True)
    r_copy.wait_recv()
    both = r_own[...] + r_sib[...]
    new_rows = 0.5 * both[:, 64:65] + 0.5 * (both[:, 0:1] / D + 1e-06)
    inverse = 1.0 / new_rows
    columns(squared * jnp.concatenate([inverse[0:12], inverse[0:12]], axis=0), 9)
    st_a[ma, 17:18, :] = jnp.sum(squared_t * inverse, axis=0, keepdims=True)
    row_part = jnp.sum(jnp.where(row[:, 0:1] < ROWS, new_rows, 0.0), axis=0, keepdims=True)
    st_a[ma, 18:24, :] = jnp.broadcast_to(row_part, (6, 128))

    def exchange(buf, me, s, r, peers):
        done = list(started)
        for d in range(1, 8):
            send(buf.at[me], buf.at[me], s.at[d], r.at[me], peers[d - 1])
        for cp in done:
            cp.wait_send()
            started.remove(cp)
        for d in (7, 1, 6, 2, 5, 3, 4):
            k = (me + d) % 8
            arrived(buf.at[k], r.at[k])
        out = buf[0]
        for k in range(1, 8):
            out += buf[k]
        return out

    def either(a, b):
        return tuple(jnp.where(c == 0, i, j) for i, j in zip(a, b))

    st_b[mb] = exchange(st_a, ma, sas, sar, [either(a, b) for a, b in zip(y_peers, z_peers)])
    st_f[c, x] = exchange(st_b, mb, sbs, sbr, [either(b, a) for a, b in zip(y_peers, z_peers)])
    done = list(started)
    started.clear()
    send(st_f.at[c, x], st_f.at[c, x], sfs.at[6], sfr.at[c, x], sib)
    for d in range(1, NX):
        send(st_f.at[c, x], st_f.at[c, x], sfs.at[d - 1], sfr.at[c, x], x_peers[d - 1])
        send(st_f.at[c, x], st_f.at[c, x], sfs.at[d + 2], sfr.at[c, x], o_peers[d - 1])

    for cp in done:
        cp.wait_send()

    def halves(own, sibling):
        return jnp.where(c == 0, own, sibling), jnp.where(c == 0, sibling, own)

    def fold(v):
        for shift in (64, 32, 16):
            v = v + pltpu.roll(v, shift, 1)
        return v

    def rows_of(v, first):
        return jnp.where(c == 0, v[first : first + 6], v[first + 6 : first + 12])

    g_copy.wait_recv()
    gt_copy.wait_recv()
    low, high = halves(g_own[...], g_sib[...])
    for h in range(2):
        gwide[0:OWN, 512 * h : 512 * (h + 1)] = rows_of(low, ROWS * h)
        gwide[0:OWN, WIDE + 512 * h : WIDE + 512 * (h + 1)] = rows_of(high, ROWS * h)
    low, high = halves(fold(gt_own[...]), fold(gt_sib[...]))
    gwide[0:OWN, 2 * WIDE :] = rows_of(jnp.where(lane < PART, low, high), 0)
    rows6 = rows_of(new_rows, 0)
    eye = lax.broadcasted_iota(jnp.int32, (OWN, 128), 0) == lax.broadcasted_iota(jnp.int32, (OWN, 128), 1)
    nr_ref[...] = jnp.sum(jnp.where(eye, rows6, 0.0), axis=0)[0:OWN]

    arrived(st_f.at[1 - c, x], sfr.at[1 - c, x])
    for d in range(1, NX):
        for cc in range(2):
            k = (x + d) % NX
            core_k = (c + cc) % 2
            arrived(st_f.at[core_k, k], sfr.at[core_k, k])
    sums = []
    for cc in range(2):
        v = st_f[cc, 0]
        for k in range(1, NX):
            v += st_f[cc, k]
        sums.append(v)
    for cc in range(2):
        for j in range(2):
            for k in range(8):
                first = WIDE * cc + 128 * k
                wide[j : j + 1, first : first + 128] = sums[cc][9 * j + k : 9 * j + k + 1]
    for j in range(2):
        low, high = (fold(v[9 * j + 8 : 9 * j + 9]) for v in sums)
        wide[j : j + 1, 2 * WIDE :] = jnp.where(lane[0:1] < PART, low, high)
    row_avg = sums[0][18:19, 0:1] / FFW
    new_cols = 0.5 * cs_ref[...].reshape(1, D) + 0.5 * (wide[0:1, 0:D] / FFW + 1e-06)
    nc_ref[...] = new_cols.reshape(D)
    total_sq = row_avg * jnp.sum(wide[1:2, 0:D] / new_cols, axis=1, keepdims=True)
    rms = jnp.sqrt(total_sq / (FFW * D))
    factor = 0.1 / jnp.maximum(1.0, rms) * jnp.sqrt(row_avg)
    scaled = gwide[0:OWN, 0:D] * (lax.rsqrt(rows6) * factor) * lax.rsqrt(new_cols)
    nw_ref[...] = (w_ref[...].astype(F32) - scaled).astype(BF16)

    for cp in started:
        cp.wait_send()


def store(a, b, c, a_out, b_out, c_out, sem):
    copies = [pltpu.make_async_copy(src, dst, sem.at[k]) for k, (src, dst) in enumerate([(a, a_out), (b, b_out), (c, c_out)])]
    for cp in copies:
        cp.start()
    for cp in copies:
        cp.wait()


def per_device(tokens, grad_out, counts, weight, row_state, col_state):
    vmem = pl.BlockSpec(memory_space=pltpu.VMEM)
    dma = pltpu.SemaphoreType.DMA

    def f32(*shape):
        return pltpu.VMEM(shape, F32)

    hbm = pl.BlockSpec(memory_space=pltpu.MemorySpace.HBM)
    results = (
        jax.ShapeDtypeStruct((OWN, D), BF16),
        jax.ShapeDtypeStruct((OWN,), F32),
        jax.ShapeDtypeStruct((D,), F32),
    )
    computed = pl.pallas_call(
        kernel,
        out_shape=tuple(pltpu.VMEM(r.shape, r.dtype) for r in results),
        in_specs=[hbm] * 6,
        out_specs=(vmem, vmem, vmem),
        scratch_shapes=[
            pltpu.VMEM((D, 256), BF16), pltpu.VMEM((256, 384), BF16), pltpu.SMEM((1,), jnp.int32),
            pltpu.VMEM((OWN, D), BF16), pltpu.SMEM((OWN,), F32), pltpu.VMEM((D,), F32), dma((6,)),
            pltpu.VMEM((2, NX, 192, 256), BF16),
            pltpu.VMEM((NX, 128, 256), BF16),
            pltpu.VMEM((64, 2048), BF16),
            pltpu.VMEM((2, 128, 2048), BF16),
            f32(NX, NZ, *UNIT), f32(NX, NZ, *UNIT), f32(NX, NZ, *UNIT),
            f32(NX, 16, 128), f32(NX, 16, 128), f32(NX, 16, 128),
            f32(2, 4, *UNIT), f32(2, NZ, *UNIT), f32(NZ, *UNIT),
            f32(NX, 16, 128), f32(NZ, 16, 128), f32(16, 128),
            f32(*UNIT), f32(*UNIT), f32(16, 128), f32(16, 128), f32(16, 128), f32(16, 128),
            f32(8, 24, 128), f32(8, 24, 128), f32(2, NX, 24, 128),
            f32(8, 2 * WIDE + 128), f32(8, 2 * WIDE + 128),
            dma((8,)), dma((8,)), dma((4,)), dma((4,)), dma((2, 4)), dma((2, 4)), dma((2, NZ)), dma((2, NZ)),
            dma((NZ,)), dma((NZ,)), dma((NX,)), dma((NX,)), dma((NZ,)), dma((NZ,)), dma((3,)), dma((3,)),
            dma((8,)), dma((8,)), dma((8,)), dma((8,)), dma((7,)), dma((2, NX)),
        ],
        compiler_params=pltpu.CompilerParams(
            collective_id=0, has_side_effects=True, vmem_limit_bytes=56 * 2**20
        ),
    )(tokens.T, grad_out, counts, weight, row_state, col_state)
    return pl.pallas_call(
        store,
        out_shape=results,
        in_specs=[vmem] * 3,
        out_specs=(hbm, hbm, hbm),
        scratch_shapes=[dma((3,))],
        compiler_params=pltpu.CompilerParams(vmem_limit_bytes=2**20),
    )(*computed)


def solution(mesh):
    placed = (
        P("dp", None),
        P("dp", "expert"),
        P("dp"),
        P(("expert", "dp"), None),
        P(("expert", "dp")),
        P(),
    )
    return jax.shard_map(
        per_device,
        mesh=mesh,
        in_specs=placed,
        out_specs=(P(("expert", "dp"), None), P(("expert", "dp")), P()),
        check_vma=False,
    )
```

```python
import jax
import jax.numpy as jnp
from jax import lax
from jax.experimental import pallas as pl
from jax.experimental.pallas import tpu as pltpu
from jax.sharding import PartitionSpec as P

D = 2080
FFW = 3072
NY, NZ, NX = 8, 8, 4
OWN = 6
ROWS = 12
WIDE = 1024
PART = 16
MAIN = 384
UNIT = (24, 512)
MESH = pl.DeviceIdType.MESH
F32 = jnp.float32
BF16 = jnp.bfloat16


def kernel(
    tok_hbm, go_hbm, cnt_hbm, w_hbm, rs_hbm, cs_hbm,
    nw_ref, nr_ref, nc_ref,
    tok_ref, go_ref, cnt_ref, w_ref, rs_ref, cs_ref, in_s, lhs, picked_t, lhs_t, rhs_t, other, acc, core_in, other_b, acc_b, core_b, bz_in, bm_in, bx_in, other_t, acc_t, core_t, d2_in, d1_in, z_in, zm_in, xt_in, zt_in,
    mine_t, g_own, g_sib, gt_own, gt_sib, r_own, r_sib, st_a, st_b, st_f, wide, gwide,
    first_s, first_r, bc_s, bc_r, bz_s, bz_r, bm_s, bm_r, bx_s, bx_r, core_s, core_r, d2_s, d2_r, d1_s, d1_r, zs, zr, zms, zmr, xts, xtr, zts, ztr, gs, gr,
    sas, sar, sbs, sbr, sfs, sfr,
):
    e = lax.axis_index("expert")
    q = lax.axis_index("dp")
    c, x, z = q % 2, (q // 2) % NX, q // (2 * NX)

    def at(ee, zz, xx, cc):
        return (ee, (zz * NX + xx) * 2 + cc)

    sib = at(e, z, x, 1 - c)
    y_peers = [at((e + d) % NY, z, x, c) for d in range(1, NY)]
    z_peers = [at(e, (z + d) % NZ, x, c) for d in range(1, NZ)]
    x_peers = [at(e, z, (x + d) % NX, c) for d in range(1, NX)]
    o_peers = [at(e, z, (x + d) % NX, 1 - c) for d in range(1, NX)]
    right, left = x_peers[0], x_peers[2]

    loads = [
        pltpu.make_async_copy(src, dst, in_s.at[k])
        for k, (src, dst) in enumerate(
            [(cnt_hbm, cnt_ref), (go_hbm, go_ref), (tok_hbm, tok_ref), (rs_hbm, rs_ref), (cs_hbm, cs_ref), (w_hbm, w_ref)]
        )
    ]
    for cp in loads:
        cp.start()
    barrier = pltpu.get_barrier_semaphore()
    everyone = [sib] + y_peers + z_peers + x_peers + o_peers
    for peer in everyone:
        pl.semaphore_signal(barrier, inc=1, device_id=peer, device_id_type=MESH)

    def remote(src, dst, s, r, peer):
        return pltpu.make_async_remote_copy(
            src_ref=src, dst_ref=dst, send_sem=s, recv_sem=r, device_id=peer, device_id_type=MESH
        )

    started = []

    def send(*args):
        cp = remote(*args)
        cp.start()
        started.append(cp)
        return cp

    def arrived(buf, sem):
        remote(buf, buf, sem, sem, sib).wait_recv()

    def nt(a, b):
        return lax.dot_general(a, b, (((1,), (1,)), ((), ())), preferred_element_type=F32)

    row = lax.broadcasted_iota(jnp.int32, (512, 384), 0)
    k = row & 15
    unit = ((row >> 4) & 7) * (NX * ROWS) + (row >> 7) * ROWS + k
    pick = (lax.broadcasted_iota(jnp.int32, (512, 384), 1) == unit) & (k < ROWS)
    pick = jnp.where(pick, 1.0, 0.0).astype(BF16)
    loads[0].wait()
    loads[1].wait()
    live = lax.broadcasted_iota(jnp.int32, (256, 384), 0) < cnt_ref[0]
    masked = jnp.where(live, go_ref[...].astype(F32), 0.0).astype(BF16)
    picked = nt(pick, masked)
    picked_t[...] = picked.astype(BF16).reshape(NX, 128, 256)
    units = picked.reshape(NX * NZ, 16, 256)
    blank = jnp.zeros((NX * NZ, 8, 256), F32)
    lhs[0] = jnp.concatenate([units, blank], axis=1).reshape(768, 256).astype(BF16).reshape(NX, 192, 256)
    moved = jnp.concatenate([blank, pltpu.roll(units, 4, 1)], axis=1)
    lhs[1] = moved.reshape(768, 256).astype(BF16).reshape(NX, 192, 256)

    def half(k, h):
        first = pl.multiple_of(WIDE * h, WIDE)
        out = nt(lhs[0, k], tok_ref[pl.ds(first, MAIN), :]) + nt(lhs[1, k], tok_ref[pl.ds(first + 512, MAIN), :])
        return out.reshape(NZ, 24, MAIN)

    def half_b(ref, h):
        first = pl.multiple_of(WIDE * h, WIDE)
        for k in range(NX):
            out = nt(lhs[0, k], tok_ref[pl.ds(first + MAIN, 128), :])
            out += nt(lhs[1, k], tok_ref[pl.ds(first + 512 + MAIN, 128), :])
            ref[:, k] = out.reshape(NZ, 24, 128)

    loads[2].wait()
    slabs = [(x + 2) % NX, (x + 1) % NX, (x + 3) % NX, x]

    def zat(d):
        return (z + d) % NZ

    def offer(j):
        k = slabs[j]
        other[k] = half(k, 1 - c)
        send(other.at[k], core_in.at[k], core_s.at[j], core_r.at[j], sib)

    def settle(j):
        k = slabs[j]
        arrived(core_in.at[k], core_r.at[j])
        acc[k] += core_in[k]

    def own(j):
        acc[slabs[j]] = half(slabs[j], c)

    halfway = ((4, 5, 6, 7), (3, 2, 1, 0))
    peer_of = (right, left)

    def skip(side, i):
        k = zat(halfway[side][i])
        arrived(core_in.at[slabs[0], k], first_r.at[4 * side + i])
        acc[slabs[0], k] += core_in[slabs[0], k]
        send(acc.at[slabs[0], k], d2_in.at[side, i], d2_s.at[side, i], d2_r.at[side, i], peer_of[side])

    def step(side, d):
        k = zat(d)
        if d in halfway[side]:
            i = halfway[side].index(d)
            arrived(d2_in.at[side, i], d2_r.at[side, i])
            acc[slabs[1 + side], k] += d2_in[side, i]
        send(acc.at[slabs[1 + side], k], d1_in.at[side, d], d1_s.at[side, d], d1_r.at[side, d], peer_of[side])

    detour = tuple(jnp.where(c == 0, a, b) for a, b in zip(z_peers[1], z_peers[5]))
    detoured = jnp.where(c == 0, zat(2), zat(6))
    relays = {3: (z_peers[0], 0), 5: (z_peers[6], 1), 4: (detour, 2)}
    directs = {1: 0, 7: 1, 2: 2, 6: 3}

    def relay(block, d, buf, ss, rr):
        peer, slot = relays[d]
        send(block, buf.at[slot], ss.at[slot], rr.at[slot], peer)

    def direct(block, d, buf, ss, rr):
        slot = directs[d]
        send(block, buf.at[slot], ss.at[slot], rr.at[slot], z_peers[d - 1])

    def settle_x(d):
        for side in range(2):
            arrived(d1_in.at[side, d], d1_r.at[side, d])
        acc[x, zat(d)] += d1_in[0, d] + d1_in[1, d]

    def deliver(d):
        settle_x(d)
        if d in relays:
            relay(acc.at[x, zat(d)], d, zm_in, zms, zmr)
        elif d:
            direct(acc.at[x, zat(d)], d, z_in, zs, zr)

    def deliver_mid():
        settle_x(2)
        settle_x(6)
        for slot, to in enumerate((zat(2), zat(6), detoured)):
            arrived(zm_in.at[slot], zmr.at[slot])
            acc[x, to] += zm_in[slot]
        for d in (2, 6):
            direct(acc.at[x, zat(d)], d, z_in, zs, zr)

    def deliver_mid_b():
        for slot, to in enumerate((zat(2), zat(6), detoured)):
            arrived(bm_in.at[slot], bm_r.at[slot])
            acc_b[to] += bm_in[slot]
        for d in (2, 6):
            direct(acc_b.at[zat(d)], d, bz_in, bz_s, bz_r)

    far_first = (4, 3, 5, 1, 7, 2, 6, 0)
    other[slabs[0]] = half(slabs[0], 1 - c)
    half_b(other_b, 1 - c)
    pl.semaphore_wait(barrier, len(everyone))
    for i in range(4):
        for side in range(2):
            k, j = zat(halfway[side][i]), 4 * side + i
            send(other.at[slabs[0], k], core_in.at[slabs[0], k], first_s.at[j], first_r.at[j], sib)
    for d in far_first:
        send(other_b.at[zat(d)], core_b.at[zat(d)], bc_s.at[d], bc_r.at[d], sib)
    own(0)
    half_b(acc_b, c)
    for i in range(2):
        skip(0, i)
        skip(1, i)
    for d in far_first:
        arrived(core_b.at[zat(d)], bc_r.at[d])
        acc_b[zat(d)] += core_b[zat(d)]
        if d in relays:
            relay(acc_b.at[zat(d)], d, bm_in, bm_s, bm_r)
        elif d in (1, 7):
            direct(acc_b.at[zat(d)], d, bz_in, bz_s, bz_r)
    skip(0, 2)
    skip(1, 2)
    offer(1)
    offer(2)
    own(1)
    settle(1)
    step(0, 3)
    own(2)
    settle(2)
    step(1, 4)
    step(0, 4)
    step(1, 3)
    offer(3)
    rhs_t[...] = jnp.zeros_like(rhs_t)
    for k in range(NZ):
        for j in range(NX):
            lhs_t[16 * j : 16 * (j + 1), 256 * k : 256 * (k + 1)] = picked_t[j, 16 * k : 16 * (k + 1), :]
        for h in range(2):
            rhs_t[h, PART * k : PART * (k + 1), 256 * k : 256 * (k + 1)] = tok_ref[
                2 * WIDE + PART * h : 2 * WIDE + PART * (h + 1), :
            ]
    other_t[...] = nt(lhs_t[...], rhs_t[1 - c]).reshape(NX, 16, 128)
    send(other_t, core_t, core_s.at[0], core_r.at[0], sib)
    acc_t[...] = nt(lhs_t[...], rhs_t[c]).reshape(NX, 16, 128)
    own(3)
    settle(3)
    step(0, 5)
    step(1, 5)
    arrived(core_t, core_r.at[0])
    acc_t[...] += core_t[...]
    for d in range(1, NX):
        k = (x + d) % NX
        send(acc_t.at[k], xt_in.at[x], xts.at[d], xtr.at[x], x_peers[d - 1])
    skip(0, 3)
    step(1, 2)
    step(0, 2)
    skip(1, 3)
    deliver_mid_b()
    deliver(4)
    deliver(3)
    step(0, 6)
    step(1, 6)
    deliver(5)
    step(0, 1)
    step(1, 1)
    step(0, 7)
    step(1, 7)
    step(0, 0)
    step(1, 0)
    xt = acc_t[x]
    for d in range(1, NX):
        k = (x + d) % NX
        arrived(xt_in.at[k], xtr.at[k])
        xt += xt_in[k]
    mine_t[...] = xt
    for d in range(1, NZ):
        send(mine_t, zt_in.at[z], zts.at[d], ztr.at[z], z_peers[d - 1])
    gathered = acc_b[z]
    for slot in range(4):
        arrived(bz_in.at[slot], bz_r.at[slot])
        gathered += bz_in[slot]
    acc_b[z] = gathered
    for d in range(1, NX):
        k = (x + d) % NX
        send(acc_b.at[z, k], bx_in.at[x], bx_s.at[d], bx_r.at[x], x_peers[d - 1])
    deliver(1)
    deliver(7)
    deliver_mid()
    deliver(0)
    total_b = acc_b[z, x]
    for d in range(1, NX):
        k = (x + d) % NX
        arrived(bx_in.at[k], bx_r.at[k])
        total_b += bx_in[k]
    total = acc[x, z]
    total_t = mine_t[...]
    for d in (4, 5, 3, 6, 2, 7, 1):
        k = zat(d)
        arrived(zt_in.at[k], ztr.at[k])
        total_t += zt_in[k]
    for slot in (0, 1, 3, 2):
        arrived(z_in.at[slot], zr.at[slot])
        total += z_in[slot]
    total = jnp.concatenate([total, total_b], axis=1)

    lane = lax.broadcasted_iota(jnp.int32, (16, 128), 1)
    row = lax.broadcasted_iota(jnp.int32, (16, 128), 0)
    tail = jnp.where((row < ROWS) & (lane // PART == z), total_t, 0.0)
    g_own[...] = total
    gt_own[...] = tail

    for cp in loads[3:]:
        cp.wait()
    squared = total * total
    squared_t = tail * tail
    state = jnp.zeros((16, 128), F32)
    for k in range(OWN):
        state = jnp.where(row == c * OWN + k, rs_ref[k], state)
    sums = jnp.sum(squared, axis=1, keepdims=True)
    sums = sums[0:16] + jnp.concatenate([sums[12:24], sums[0:4]], axis=0) + jnp.sum(squared_t, axis=1, keepdims=True)
    r_own[...] = jnp.where(lane < 64, sums, state)
    r_copy = send(r_own, r_sib, gs.at[0], gr.at[0], sib)
    g_copy = send(g_own, g_sib, gs.at[1], gr.at[1], sib)
    gt_copy = send(gt_own, gt_sib, gs.at[2], gr.at[2], sib)

    row24 = lax.broadcasted_iota(jnp.int32, (24, 1), 0)

    def columns(values, k):
        for h in range(2):
            part = jnp.sum(jnp.where((row24 < ROWS) == (h == 0), values, 0.0), axis=0, keepdims=True)
            for j in range(4):
                st_a[ma, k + 4 * h + j : k + 4 * h + j + 1, :] = part[:, 128 * j : 128 * (j + 1)]

    ma = jnp.where(c == 0, e, z)
    mb = jnp.where(c == 0, z, e)
    columns(squared, 0)
    st_a[ma, 8:9, :] = jnp.sum(squared_t, axis=0, keepdims=True)
    r_copy.wait_recv()
    both = r_own[...] + r_sib[...]
    new_rows = 0.5 * both[:, 64:65] + 0.5 * (both[:, 0:1] / D + 1e-06)
    inverse = 1.0 / new_rows
    columns(squared * jnp.concatenate([inverse[0:12], inverse[0:12]], axis=0), 9)
    st_a[ma, 17:18, :] = jnp.sum(squared_t * inverse, axis=0, keepdims=True)
    row_part = jnp.sum(jnp.where(row[:, 0:1] < ROWS, new_rows, 0.0), axis=0, keepdims=True)
    st_a[ma, 18:24, :] = jnp.broadcast_to(row_part, (6, 128))

    def exchange(buf, me, s, r, peers):
        done = list(started)
        for d in range(1, 8):
            send(buf.at[me], buf.at[me], s.at[d], r.at[me], peers[d - 1])
        for cp in done:
            cp.wait_send()
            started.remove(cp)
        for d in (7, 1, 6, 2, 5, 3, 4):
            k = (me + d) % 8
            arrived(buf.at[k], r.at[k])
        out = buf[0]
        for k in range(1, 8):
            out += buf[k]
        return out

    def either(a, b):
        return tuple(jnp.where(c == 0, i, j) for i, j in zip(a, b))

    st_b[mb] = exchange(st_a, ma, sas, sar, [either(a, b) for a, b in zip(y_peers, z_peers)])
    st_f[c, x] = exchange(st_b, mb, sbs, sbr, [either(b, a) for a, b in zip(y_peers, z_peers)])
    done = list(started)
    started.clear()
    send(st_f.at[c, x], st_f.at[c, x], sfs.at[6], sfr.at[c, x], sib)
    for d in range(1, NX):
        send(st_f.at[c, x], st_f.at[c, x], sfs.at[d - 1], sfr.at[c, x], x_peers[d - 1])
        send(st_f.at[c, x], st_f.at[c, x], sfs.at[d + 2], sfr.at[c, x], o_peers[d - 1])

    for cp in done:
        cp.wait_send()

    def halves(own, sibling):
        return jnp.where(c == 0, own, sibling), jnp.where(c == 0, sibling, own)

    def fold(v):
        for shift in (64, 32, 16):
            v = v + pltpu.roll(v, shift, 1)
        return v

    def rows_of(v, first):
        return jnp.where(c == 0, v[first : first + 6], v[first + 6 : first + 12])

    g_copy.wait_recv()
    gt_copy.wait_recv()
    low, high = halves(g_own[...], g_sib[...])
    for h in range(2):
        gwide[0:OWN, 512 * h : 512 * (h + 1)] = rows_of(low, ROWS * h)
        gwide[0:OWN, WIDE + 512 * h : WIDE + 512 * (h + 1)] = rows_of(high, ROWS * h)
    low, high = halves(fold(gt_own[...]), fold(gt_sib[...]))
    gwide[0:OWN, 2 * WIDE :] = rows_of(jnp.where(lane < PART, low, high), 0)
    rows6 = rows_of(new_rows, 0)
    eye = lax.broadcasted_iota(jnp.int32, (OWN, 128), 0) == lax.broadcasted_iota(jnp.int32, (OWN, 128), 1)
    nr_ref[...] = jnp.sum(jnp.where(eye, rows6, 0.0), axis=0)[0:OWN]

    arrived(st_f.at[1 - c, x], sfr.at[1 - c, x])
    for d in range(1, NX):
        for cc in range(2):
            k = (x + d) % NX
            core_k = (c + cc) % 2
            arrived(st_f.at[core_k, k], sfr.at[core_k, k])
    sums = []
    for cc in range(2):
        v = st_f[cc, 0]
        for k in range(1, NX):
            v += st_f[cc, k]
        sums.append(v)
    for cc in range(2):
        for j in range(2):
            for k in range(8):
                first = WIDE * cc + 128 * k
                wide[j : j + 1, first : first + 128] = sums[cc][9 * j + k : 9 * j + k + 1]
    for j in range(2):
        low, high = (fold(v[9 * j + 8 : 9 * j + 9]) for v in sums)
        wide[j : j + 1, 2 * WIDE :] = jnp.where(lane[0:1] < PART, low, high)
    row_avg = sums[0][18:19, 0:1] / FFW
    new_cols = 0.5 * cs_ref[...].reshape(1, D) + 0.5 * (wide[0:1, 0:D] / FFW + 1e-06)
    nc_ref[...] = new_cols.reshape(D)
    total_sq = row_avg * jnp.sum(wide[1:2, 0:D] / new_cols, axis=1, keepdims=True)
    rms = jnp.sqrt(total_sq / (FFW * D))
    factor = 0.1 / jnp.maximum(1.0, rms) * jnp.sqrt(row_avg)
    scaled = gwide[0:OWN, 0:D] * (lax.rsqrt(rows6) * factor) * lax.rsqrt(new_cols)
    nw_ref[...] = (w_ref[...].astype(F32) - scaled).astype(BF16)

    for cp in started:
        cp.wait_send()


def store(a, b, c, a_out, b_out, c_out, sem):
    copies = [pltpu.make_async_copy(src, dst, sem.at[k]) for k, (src, dst) in enumerate([(a, a_out), (b, b_out), (c, c_out)])]
    for cp in copies:
        cp.start()
    for cp in copies:
        cp.wait()


def per_device(tokens, grad_out, counts, weight, row_state, col_state):
    vmem = pl.BlockSpec(memory_space=pltpu.VMEM)
    dma = pltpu.SemaphoreType.DMA

    def f32(*shape):
        return pltpu.VMEM(shape, F32)

    hbm = pl.BlockSpec(memory_space=pltpu.MemorySpace.HBM)
    results = (
        jax.ShapeDtypeStruct((OWN, D), BF16),
        jax.ShapeDtypeStruct((OWN,), F32),
        jax.ShapeDtypeStruct((D,), F32),
    )
    computed = pl.pallas_call(
        kernel,
        out_shape=tuple(pltpu.VMEM(r.shape, r.dtype) for r in results),
        in_specs=[hbm] * 6,
        out_specs=(vmem, vmem, vmem),
        scratch_shapes=[
            pltpu.VMEM((D, 256), BF16), pltpu.VMEM((256, 384), BF16), pltpu.SMEM((1,), jnp.int32),
            pltpu.VMEM((OWN, D), BF16), pltpu.SMEM((OWN,), F32), pltpu.VMEM((D,), F32), dma((6,)),
            pltpu.VMEM((2, NX, 192, 256), BF16),
            pltpu.VMEM((NX, 128, 256), BF16),
            pltpu.VMEM((64, 2048), BF16),
            pltpu.VMEM((2, 128, 2048), BF16),
            f32(NX, NZ, 24, MAIN), f32(NX, NZ, 24, MAIN), f32(NX, NZ, 24, MAIN),
            f32(NZ, NX, 24, 128), f32(NZ, NX, 24, 128), f32(NZ, NX, 24, 128), f32(4, NX, 24, 128), f32(3, NX, 24, 128), f32(NX, 24, 128),
            f32(NX, 16, 128), f32(NX, 16, 128), f32(NX, 16, 128),
            f32(2, 4, 24, MAIN), f32(2, NZ, 24, MAIN), f32(4, 24, MAIN), f32(3, 24, MAIN),
            f32(NX, 16, 128), f32(NZ, 16, 128), f32(16, 128),
            f32(*UNIT), f32(*UNIT), f32(16, 128), f32(16, 128), f32(16, 128), f32(16, 128),
            f32(8, 24, 128), f32(8, 24, 128), f32(2, NX, 24, 128),
            f32(8, 2 * WIDE + 128), f32(8, 2 * WIDE + 128),
            dma((8,)), dma((8,)), dma((8,)), dma((8,)), dma((4,)), dma((4,)), dma((3,)), dma((3,)), dma((NX,)), dma((NX,)),
            dma((4,)), dma((4,)), dma((2, 4)), dma((2, 4)), dma((2, NZ)), dma((2, NZ)),
            dma((4,)), dma((4,)), dma((3,)), dma((3,)), dma((NX,)), dma((NX,)), dma((NZ,)), dma((NZ,)), dma((3,)), dma((3,)),
            dma((8,)), dma((8,)), dma((8,)), dma((8,)), dma((7,)), dma((2, NX)),
        ],
        compiler_params=pltpu.CompilerParams(
            collective_id=0, has_side_effects=True, vmem_limit_bytes=56 * 2**20
        ),
    )(tokens.T, grad_out, counts, weight, row_state, col_state)
    return pl.pallas_call(
        store,
        out_shape=results,
        in_specs=[vmem] * 3,
        out_specs=(hbm, hbm, hbm),
        scratch_shapes=[dma((3,))],
        compiler_params=pltpu.CompilerParams(vmem_limit_bytes=2**20),
    )(*computed)


def solution(mesh):
    placed = (
        P("dp", None),
        P("dp", "expert"),
        P("dp"),
        P(("expert", "dp"), None),
        P(("expert", "dp")),
        P(),
    )
    return jax.shard_map(
        per_device,
        mesh=mesh,
        in_specs=placed,
        out_specs=(P(("expert", "dp"), None), P(("expert", "dp")), P()),
        check_vma=False,
    )
```

```python
import jax
import jax.numpy as jnp
from jax import lax
from jax.experimental import pallas as pl
from jax.experimental.pallas import tpu as pltpu
from jax.sharding import PartitionSpec as P

D = 2080
FFW = 3072
NY, NZ, NX = 8, 8, 4
OWN = 6
ROWS = 12
WIDE = 1024
PART = 16
MAIN = 384
UNIT = (24, 512)
STATS = 17
MESH = pl.DeviceIdType.MESH
F32 = jnp.float32
BF16 = jnp.bfloat16


def kernel(
    tok_hbm, go_hbm, cnt_hbm, w_hbm, rs_hbm, cs_hbm,
    nw_ref, nr_ref, nc_ref,
    tok_ref, go_ref, cnt_ref, w_ref, rs_ref, cs_ref, in_s, lhs, picked_t, lhs_t, rhs_t, other, acc, core_in, other_b, acc_b, core_b, bz_in, bm_in, bx_in, other_t, acc_t, core_t, d2_in, d1_in, z_in, zm_in, xt_in, zt_in,
    mine_t, g_own, g_sib, gt_own, gt_sib, r_own, r_sib, st_a, st_b, st_f, wide, gwide,
    first_s, first_r, bc_s, bc_r, bz_s, bz_r, bm_s, bm_r, bx_s, bx_r, core_s, core_r, d2_s, d2_r, d1_s, d1_r, zs, zr, zms, zmr, xts, xtr, zts, ztr, gs, gr,
    sas, sar, sbs, sbr, sfs, sfr,
):
    e = lax.axis_index("expert")
    q = lax.axis_index("dp")
    c, x, z = q % 2, (q // 2) % NX, q // (2 * NX)

    def at(ee, zz, xx, cc):
        return (ee, (zz * NX + xx) * 2 + cc)

    sib = at(e, z, x, 1 - c)
    y_peers = [at((e + d) % NY, z, x, c) for d in range(1, NY)]
    z_peers = [at(e, (z + d) % NZ, x, c) for d in range(1, NZ)]
    x_peers = [at(e, z, (x + d) % NX, c) for d in range(1, NX)]
    o_peers = [at(e, z, (x + d) % NX, 1 - c) for d in range(1, NX)]
    right, left = x_peers[0], x_peers[2]

    loads = [
        pltpu.make_async_copy(src, dst, in_s.at[k])
        for k, (src, dst) in enumerate(
            [(cnt_hbm, cnt_ref), (go_hbm, go_ref), (tok_hbm, tok_ref), (rs_hbm, rs_ref), (cs_hbm, cs_ref), (w_hbm, w_ref)]
        )
    ]
    for cp in loads:
        cp.start()
    barrier = pltpu.get_barrier_semaphore()
    everyone = [sib] + y_peers + z_peers + x_peers + o_peers
    for peer in everyone:
        pl.semaphore_signal(barrier, inc=1, device_id=peer, device_id_type=MESH)

    def remote(src, dst, s, r, peer):
        return pltpu.make_async_remote_copy(
            src_ref=src, dst_ref=dst, send_sem=s, recv_sem=r, device_id=peer, device_id_type=MESH
        )

    started = []

    def send(*args):
        cp = remote(*args)
        cp.start()
        started.append(cp)
        return cp

    def arrived(buf, sem):
        remote(buf, buf, sem, sem, sib).wait_recv()

    def nt(a, b):
        return lax.dot_general(a, b, (((1,), (1,)), ((), ())), preferred_element_type=F32)

    row = lax.broadcasted_iota(jnp.int32, (512, 384), 0)
    k = row & 15
    unit = ((row >> 4) & 7) * (NX * ROWS) + (row >> 7) * ROWS + k
    pick = (lax.broadcasted_iota(jnp.int32, (512, 384), 1) == unit) & (k < ROWS)
    pick = jnp.where(pick, 1.0, 0.0).astype(BF16)
    loads[0].wait()
    loads[1].wait()
    live = lax.broadcasted_iota(jnp.int32, (256, 384), 0) < cnt_ref[0]
    masked = jnp.where(live, go_ref[...].astype(F32), 0.0).astype(BF16)
    picked = nt(pick, masked)
    picked_t[...] = picked.astype(BF16).reshape(NX, 128, 256)
    units = picked.reshape(NX * NZ, 16, 256)
    blank = jnp.zeros((NX * NZ, 8, 256), F32)
    lhs[0] = jnp.concatenate([units, blank], axis=1).reshape(768, 256).astype(BF16).reshape(NX, 192, 256)
    moved = jnp.concatenate([blank, pltpu.roll(units[:, 8:16], 4, 1), units[:, 0:8]], axis=1)
    lhs[1] = moved.reshape(768, 256).astype(BF16).reshape(NX, 192, 256)

    def half(k, h):
        first = pl.multiple_of(WIDE * h, WIDE)
        out = nt(lhs[0, k], tok_ref[pl.ds(first, MAIN), :]) + nt(lhs[1, k], tok_ref[pl.ds(first + 512, MAIN), :])
        return out.reshape(NZ, 24, MAIN)

    def half_b(ref, h):
        first = pl.multiple_of(WIDE * h, WIDE)
        for k in range(NX):
            out = nt(lhs[0, k], tok_ref[pl.ds(first + MAIN, 128), :])
            out += nt(lhs[1, k], tok_ref[pl.ds(first + 512 + MAIN, 128), :])
            ref[:, k] = out.reshape(NZ, 24, 128)

    loads[2].wait()
    slabs = [(x + 2) % NX, (x + 1) % NX, (x + 3) % NX, x]

    def zat(d):
        return (z + d) % NZ

    def offer(j):
        k = slabs[j]
        other[k] = half(k, 1 - c)
        send(other.at[k], core_in.at[k], core_s.at[j], core_r.at[j], sib)

    def settle(j):
        k = slabs[j]
        arrived(core_in.at[k], core_r.at[j])
        acc[k] += core_in[k]

    def own(j):
        acc[slabs[j]] = half(slabs[j], c)

    halfway = ((4, 5, 6, 7), (3, 2, 1, 0))
    peer_of = (right, left)

    def skip(side, i):
        k = zat(halfway[side][i])
        arrived(core_in.at[slabs[0], k], first_r.at[4 * side + i])
        acc[slabs[0], k] += core_in[slabs[0], k]
        send(acc.at[slabs[0], k], d2_in.at[side, i], d2_s.at[side, i], d2_r.at[side, i], peer_of[side])

    def step(side, d):
        k = zat(d)
        if d in halfway[side]:
            i = halfway[side].index(d)
            arrived(d2_in.at[side, i], d2_r.at[side, i])
            acc[slabs[1 + side], k] += d2_in[side, i]
        send(acc.at[slabs[1 + side], k], d1_in.at[side, d], d1_s.at[side, d], d1_r.at[side, d], peer_of[side])

    detour = tuple(jnp.where(c == 0, a, b) for a, b in zip(z_peers[1], z_peers[5]))
    detoured = jnp.where(c == 0, zat(2), zat(6))
    relays = {3: (z_peers[0], 0), 5: (z_peers[6], 1), 4: (detour, 2)}
    directs = {1: 0, 7: 1, 2: 2, 6: 3}

    def relay(block, d, buf, ss, rr):
        peer, slot = relays[d]
        send(block, buf.at[slot], ss.at[slot], rr.at[slot], peer)

    def direct(block, d, buf, ss, rr):
        slot = directs[d]
        send(block, buf.at[slot], ss.at[slot], rr.at[slot], z_peers[d - 1])

    def settle_x(d):
        for side in range(2):
            arrived(d1_in.at[side, d], d1_r.at[side, d])
        acc[x, zat(d)] += d1_in[0, d] + d1_in[1, d]

    def deliver(d):
        settle_x(d)
        if d in relays:
            relay(acc.at[x, zat(d)], d, zm_in, zms, zmr)
        elif d:
            direct(acc.at[x, zat(d)], d, z_in, zs, zr)

    def deliver_mid():
        settle_x(2)
        settle_x(6)
        for slot, to in enumerate((zat(2), zat(6), detoured)):
            arrived(zm_in.at[slot], zmr.at[slot])
            acc[x, to] += zm_in[slot]
        for d in (2, 6):
            direct(acc.at[x, zat(d)], d, z_in, zs, zr)

    def deliver_mid_b():
        for slot, to in enumerate((zat(2), zat(6), detoured)):
            arrived(bm_in.at[slot], bm_r.at[slot])
            acc_b[to] += bm_in[slot]
        for d in (2, 6):
            direct(acc_b.at[zat(d)], d, bz_in, bz_s, bz_r)

    far_first = (4, 3, 5, 1, 7, 2, 6, 0)
    other[slabs[0]] = half(slabs[0], 1 - c)
    pl.semaphore_wait(barrier, len(everyone))
    for i in range(4):
        for side in range(2):
            k, j = zat(halfway[side][i]), 4 * side + i
            send(other.at[slabs[0], k], core_in.at[slabs[0], k], first_s.at[j], first_r.at[j], sib)
    own(0)
    half_b(other_b, 1 - c)
    for d in far_first:
        send(other_b.at[zat(d)], core_b.at[zat(d)], bc_s.at[d], bc_r.at[d], sib)
    for i in range(2):
        skip(0, i)
        skip(1, i)
    half_b(acc_b, c)
    for d in far_first:
        arrived(core_b.at[zat(d)], bc_r.at[d])
        acc_b[zat(d)] += core_b[zat(d)]
        if d in relays:
            relay(acc_b.at[zat(d)], d, bm_in, bm_s, bm_r)
        elif d in (1, 7):
            direct(acc_b.at[zat(d)], d, bz_in, bz_s, bz_r)
    skip(0, 2)
    skip(1, 2)
    offer(1)
    offer(2)
    own(1)
    settle(1)
    step(0, 3)
    own(2)
    settle(2)
    step(1, 4)
    step(0, 4)
    step(1, 3)
    offer(3)
    rhs_t[...] = jnp.zeros_like(rhs_t)
    for k in range(NZ):
        for j in range(NX):
            lhs_t[16 * j : 16 * (j + 1), 256 * k : 256 * (k + 1)] = picked_t[j, 16 * k : 16 * (k + 1), :]
        for h in range(2):
            rhs_t[h, PART * k : PART * (k + 1), 256 * k : 256 * (k + 1)] = tok_ref[
                2 * WIDE + PART * h : 2 * WIDE + PART * (h + 1), :
            ]
    other_t[...] = nt(lhs_t[...], rhs_t[1 - c]).reshape(NX, 16, 128)
    send(other_t, core_t, core_s.at[0], core_r.at[0], sib)
    acc_t[...] = nt(lhs_t[...], rhs_t[c]).reshape(NX, 16, 128)
    own(3)
    settle(3)
    step(0, 5)
    step(1, 5)
    arrived(core_t, core_r.at[0])
    acc_t[...] += core_t[...]
    for d in range(1, NX):
        k = (x + d) % NX
        send(acc_t.at[k], xt_in.at[x], xts.at[d], xtr.at[x], x_peers[d - 1])
    skip(0, 3)
    step(1, 2)
    step(0, 2)
    skip(1, 3)
    deliver_mid_b()
    deliver(4)
    deliver(3)
    step(0, 6)
    step(1, 6)
    deliver(5)
    step(0, 1)
    step(1, 1)
    step(0, 7)
    step(1, 7)
    step(0, 0)
    step(1, 0)
    xt = acc_t[x]
    for d in range(1, NX):
        k = (x + d) % NX
        arrived(xt_in.at[k], xtr.at[k])
        xt += xt_in[k]
    mine_t[...] = xt
    for d in range(1, NZ):
        send(mine_t, zt_in.at[z], zts.at[d], ztr.at[z], z_peers[d - 1])
    gathered = acc_b[z]
    for slot in range(4):
        arrived(bz_in.at[slot], bz_r.at[slot])
        gathered += bz_in[slot]
    acc_b[z] = gathered
    for d in range(1, NX):
        k = (x + d) % NX
        send(acc_b.at[z, k], bx_in.at[x], bx_s.at[d], bx_r.at[x], x_peers[d - 1])
    deliver(1)
    deliver(7)
    deliver_mid()
    deliver(0)
    total_b = acc_b[z, x]
    for d in range(1, NX):
        k = (x + d) % NX
        arrived(bx_in.at[k], bx_r.at[k])
        total_b += bx_in[k]
    total = acc[x, z]
    total_t = mine_t[...]
    for d in (4, 5, 3, 6, 2, 7, 1):
        k = zat(d)
        arrived(zt_in.at[k], ztr.at[k])
        total_t += zt_in[k]
    for slot in (0, 1, 3, 2):
        arrived(z_in.at[slot], zr.at[slot])
        total += z_in[slot]
    total = jnp.concatenate([total, total_b], axis=1)

    lane = lax.broadcasted_iota(jnp.int32, (16, 128), 1)
    row = lax.broadcasted_iota(jnp.int32, (16, 128), 0)
    tail = jnp.where((row < ROWS) & (lane < PART), pltpu.roll(total_t, (8 - z) % 8 * PART, 1), 0.0)
    tail_up = jnp.where((row < ROWS) & (lane >= PART) & (lane < 2 * PART), pltpu.roll(total_t, (9 - z) % 8 * PART, 1), 0.0)
    g_own[...] = total
    gt_own[...] = tail

    for cp in loads[3:]:
        cp.wait()
    squared = total * total
    squared_t = tail * tail
    squared_up = tail_up * tail_up
    state = jnp.zeros((16, 128), F32)
    for k in range(OWN):
        state = jnp.where(jnp.where(row < ROWS, row, row - 4) == c * OWN + k, rs_ref[k], state)
    sums = jnp.sum(squared, axis=1, keepdims=True)
    sums_t = jnp.sum(squared_t, axis=1, keepdims=True)
    upper = jnp.broadcast_to(sums[8:16] + sums_t[8:16], (8, 128))
    r_own[0:8, :] = jnp.where(lane[0:8] < 64, sums[0:8] + sums[16:24] + sums_t[0:8], state[0:8])
    r_own[8:16, :] = jnp.where(lane[0:8] < 64, upper + pltpu.roll(upper, 4, 0), state[8:16])
    r_copy = send(r_own, r_sib, gs.at[0], gr.at[0], sib)
    g_copy = send(g_own, g_sib, gs.at[1], gr.at[1], sib)
    gt_copy = send(gt_own, gt_sib, gs.at[2], gr.at[2], sib)

    row24 = lax.broadcasted_iota(jnp.int32, (24, 1), 0)

    def columns(values, k):
        for h in range(2):
            part = jnp.sum(jnp.where((row24 < ROWS) == (h == 0), values, 0.0), axis=0, keepdims=True)
            for j in range(4):
                st_a[ma, k + 4 * h + j] = part[:, 128 * j : 128 * (j + 1)]

    ma = jnp.where(c == 0, e, z)
    mb = jnp.where(c == 0, z, e)
    columns(squared, 0)
    tail_c = jnp.sum(squared_t, axis=0, keepdims=True)
    r_copy.wait_recv()
    both = r_own[...] + r_sib[...]
    new_rows = 0.5 * both[:, 64:65] + 0.5 * (both[:, 0:1] / D + 1e-06)
    inverse = 1.0 / new_rows
    columns(squared * jnp.concatenate([inverse, inverse[0:8]], axis=0), 8)
    row_part = jnp.sum(jnp.where(row[:, 0:1] < ROWS, new_rows, 0.0), axis=0, keepdims=True)
    tail_s = jnp.sum(squared_up * inverse, axis=0, keepdims=True)
    st_a[ma, 16] = jnp.where(lane[0:1] < 2 * PART, tail_c + tail_s, row_part)

    def exchange(buf, me, s, r, peers):
        done = list(started)
        for d in (4, 3, 5, 2, 6, 1, 7):
            send(buf.at[me], buf.at[me], s.at[d], r.at[me], peers[d - 1])
        for cp in done:
            cp.wait_send()
            started.remove(cp)
        for d in (7, 1, 6, 2, 5, 3, 4):
            k = (me + d) % 8
            arrived(buf.at[k], r.at[k])
        out = buf[0]
        for k in range(1, 8):
            out += buf[k]
        return out

    def either(a, b):
        return tuple(jnp.where(c == 0, i, j) for i, j in zip(a, b))

    st_b[mb] = exchange(st_a, ma, sas, sar, [either(a, b) for a, b in zip(y_peers, z_peers)])
    st_f[c, x] = exchange(st_b, mb, sbs, sbr, [either(b, a) for a, b in zip(y_peers, z_peers)])
    done = list(started)
    started.clear()
    for d in (2, 1, 3):
        send(st_f.at[c, x], st_f.at[c, x], sfs.at[d - 1], sfr.at[c, x], x_peers[d - 1])
        send(st_f.at[c, x], st_f.at[c, x], sfs.at[d + 2], sfr.at[c, x], o_peers[d - 1])
    send(st_f.at[c, x], st_f.at[c, x], sfs.at[6], sfr.at[c, x], sib)

    for cp in done:
        cp.wait_send()

    def halves(own, sibling):
        return jnp.where(c == 0, own, sibling), jnp.where(c == 0, sibling, own)

    def rows_of(v, first):
        return jnp.where(c == 0, v[first : first + 6], v[first + 6 : first + 12])

    g_copy.wait_recv()
    gt_copy.wait_recv()
    low, high = halves(g_own[...], g_sib[...])
    for h in range(2):
        for first, v in ((512 * h, low), (WIDE + 512 * h, high)):
            v = jnp.concatenate([v[16:24], v[12:16]], axis=0) if h else v
            gwide[0:OWN, first : first + 512] = rows_of(v, 0)
    low, high = halves(gt_own[...], gt_sib[...])
    gwide[0:OWN, 2 * WIDE :] = rows_of(low + pltpu.roll(high, PART, 1), 0)
    rows6 = rows_of(new_rows, 0)
    gwide[0:OWN, :] *= lax.rsqrt(rows6)
    eye = lax.broadcasted_iota(jnp.int32, (OWN, 128), 0) == lax.broadcasted_iota(jnp.int32, (OWN, 128), 1)
    nr_ref[...] = jnp.sum(jnp.where(eye, rows6, 0.0), axis=0)[0:OWN]

    arrived(st_f.at[1 - c, x], sfr.at[1 - c, x])
    for d in range(1, NX):
        for cc in range(2):
            k = (x + d) % NX
            core_k = (c + cc) % 2
            arrived(st_f.at[core_k, k], sfr.at[core_k, k])
    sums = []
    for cc in range(2):
        v = st_f[cc, 0]
        for k in range(1, NX):
            v += st_f[cc, k]
        sums.append(v)
    for cc in range(2):
        for j in range(2):
            for k in range(8):
                first = WIDE * cc + 128 * k
                wide[j : j + 1, first : first + 128] = sums[cc][8 * j + k]
    low, high = sums[0][16], sums[1][16]
    wide[0:1, 2 * WIDE :] = jnp.where(lane[0:1] < PART, low, pltpu.roll(high, PART, 1))
    wide[1:2, 2 * WIDE :] = jnp.where(lane[0:1] < PART, pltpu.roll(low, 128 - PART, 1), high)
    row_avg = sums[0][16][:, 2 * PART : 2 * PART + 1] / FFW
    new_cols = 0.5 * cs_ref[...].reshape(1, D) + 0.5 * (wide[0:1, 0:D] / FFW + 1e-06)
    nc_ref[...] = new_cols.reshape(D)
    total_sq = row_avg * jnp.sum(wide[1:2, 0:D] / new_cols, axis=1, keepdims=True)
    rms = jnp.sqrt(total_sq / (FFW * D))
    factor = 0.1 / jnp.maximum(1.0, rms) * jnp.sqrt(row_avg)
    scaled = gwide[0:OWN, 0:D] * (lax.rsqrt(new_cols) * factor)
    nw_ref[...] = (w_ref[...].astype(F32) - scaled).astype(BF16)

    for cp in started:
        cp.wait_send()


def store(a, b, c, a_out, b_out, c_out, sem):
    copies = [pltpu.make_async_copy(src, dst, sem.at[k]) for k, (src, dst) in enumerate([(a, a_out), (b, b_out), (c, c_out)])]
    for cp in copies:
        cp.start()
    for cp in copies:
        cp.wait()


def per_device(tokens, grad_out, counts, weight, row_state, col_state):
    vmem = pl.BlockSpec(memory_space=pltpu.VMEM)
    dma = pltpu.SemaphoreType.DMA

    def f32(*shape):
        return pltpu.VMEM(shape, F32)

    hbm = pl.BlockSpec(memory_space=pltpu.MemorySpace.HBM)
    results = (
        jax.ShapeDtypeStruct((OWN, D), BF16),
        jax.ShapeDtypeStruct((OWN,), F32),
        jax.ShapeDtypeStruct((D,), F32),
    )
    computed = pl.pallas_call(
        kernel,
        out_shape=tuple(pltpu.VMEM(r.shape, r.dtype) for r in results),
        in_specs=[hbm] * 6,
        out_specs=(vmem, vmem, vmem),
        scratch_shapes=[
            pltpu.VMEM((D, 256), BF16), pltpu.VMEM((256, 384), BF16), pltpu.SMEM((1,), jnp.int32),
            pltpu.VMEM((OWN, D), BF16), pltpu.SMEM((OWN,), F32), pltpu.VMEM((D,), F32), dma((6,)),
            pltpu.VMEM((2, NX, 192, 256), BF16),
            pltpu.VMEM((NX, 128, 256), BF16),
            pltpu.VMEM((64, 2048), BF16),
            pltpu.VMEM((2, 128, 2048), BF16),
            f32(NX, NZ, 24, MAIN), f32(NX, NZ, 24, MAIN), f32(NX, NZ, 24, MAIN),
            f32(NZ, NX, 24, 128), f32(NZ, NX, 24, 128), f32(NZ, NX, 24, 128), f32(4, NX, 24, 128), f32(3, NX, 24, 128), f32(NX, 24, 128),
            f32(NX, 16, 128), f32(NX, 16, 128), f32(NX, 16, 128),
            f32(2, 4, 24, MAIN), f32(2, NZ, 24, MAIN), f32(4, 24, MAIN), f32(3, 24, MAIN),
            f32(NX, 16, 128), f32(NZ, 16, 128), f32(16, 128),
            f32(*UNIT), f32(*UNIT), f32(16, 128), f32(16, 128), f32(16, 128), f32(16, 128),
            f32(8, STATS, 1, 128), f32(8, STATS, 1, 128), f32(2, NX, STATS, 1, 128),
            f32(8, 2 * WIDE + 128), f32(8, 2 * WIDE + 128),
            dma((8,)), dma((8,)), dma((8,)), dma((8,)), dma((4,)), dma((4,)), dma((3,)), dma((3,)), dma((NX,)), dma((NX,)),
            dma((4,)), dma((4,)), dma((2, 4)), dma((2, 4)), dma((2, NZ)), dma((2, NZ)),
            dma((4,)), dma((4,)), dma((3,)), dma((3,)), dma((NX,)), dma((NX,)), dma((NZ,)), dma((NZ,)), dma((3,)), dma((3,)),
            dma((8,)), dma((8,)), dma((8,)), dma((8,)), dma((7,)), dma((2, NX)),
        ],
        compiler_params=pltpu.CompilerParams(
            collective_id=0, has_side_effects=True, vmem_limit_bytes=56 * 2**20
        ),
    )(tokens.T, grad_out, counts, weight, row_state, col_state)
    return pl.pallas_call(
        store,
        out_shape=results,
        in_specs=[vmem] * 3,
        out_specs=(hbm, hbm, hbm),
        scratch_shapes=[dma((3,))],
        compiler_params=pltpu.CompilerParams(vmem_limit_bytes=2**20),
    )(*computed)


def solution(mesh):
    placed = (
        P("dp", None),
        P("dp", "expert"),
        P("dp"),
        P(("expert", "dp"), None),
        P(("expert", "dp")),
        P(),
    )
    return jax.shard_map(
        per_device,
        mesh=mesh,
        in_specs=placed,
        out_specs=(P(("expert", "dp"), None), P(("expert", "dp")), P()),
        check_vma=False,
    )
```

```python
import jax
import jax.numpy as jnp
from jax import lax
from jax.experimental import pallas as pl
from jax.experimental.pallas import tpu as pltpu
from jax.sharding import PartitionSpec as P

D = 2080
FFW = 3072
NY, NZ, NX = 8, 8, 4
OWN = 6
ROWS = 12
WIDE = 1024
PART = 16
MAIN = 384
UNIT = (24, 512)
STATS = 17
MESH = pl.DeviceIdType.MESH
F32 = jnp.float32
BF16 = jnp.bfloat16


def kernel(
    tok_hbm, go_hbm, cnt_hbm, w_hbm, rs_hbm, cs_hbm,
    nw_ref, nr_ref, nc_ref,
    tok_ref, go_ref, cnt_ref, w_ref, rs_ref, cs_ref, in_s, lhs, picked_t, lhs_t, rhs_t, other, acc, core_in, other_b, acc_b, core_b, bz_in, bm_in, bx_in, other_t, acc_t, core_t, d2_in, d1_in, z_in, zm_in, xt_in, zt_in,
    mine_t, g_own, g_sib, gt_own, gt_sib, r_own, r_sib, st_a, st_b, st_f, wide, gwide,
    core_s, first_r, core_r, bc_s, bc_r, bz_s, bz_r, bm_s, bm_r, bx_s, bx_r, d2_s, d2_r, d1_s, d1_r,
    zs, zr, zms, zmr, xts, xtr, zts, ztr, gs, gr, sas, sar, sbs, sbr, sfs, sfr,
):
    e = lax.axis_index("expert")
    q = lax.axis_index("dp")
    c, x, z = q % 2, (q // 2) % NX, q // (2 * NX)

    def at(ee, zz, xx, cc):
        return (ee, (zz * NX + xx) * 2 + cc)

    sib = at(e, z, x, 1 - c)
    y_peers = [at((e + d) % NY, z, x, c) for d in range(1, NY)]
    z_peers = [at(e, (z + d) % NZ, x, c) for d in range(1, NZ)]
    x_peers = [at(e, z, (x + d) % NX, c) for d in range(1, NX)]
    o_peers = [at(e, z, (x + d) % NX, 1 - c) for d in range(1, NX)]
    right, left = x_peers[0], x_peers[2]

    loads = [
        pltpu.make_async_copy(src, dst, in_s.at[k])
        for k, (src, dst) in enumerate(
            [(cnt_hbm, cnt_ref), (go_hbm, go_ref), (tok_hbm, tok_ref), (rs_hbm, rs_ref), (cs_hbm, cs_ref), (w_hbm, w_ref)]
        )
    ]
    for cp in loads:
        cp.start()
    barrier = pltpu.get_barrier_semaphore()
    everyone = [sib] + y_peers + z_peers + x_peers + o_peers
    for peer in everyone:
        pl.semaphore_signal(barrier, inc=1, device_id=peer, device_id_type=MESH)

    def remote(src, dst, s, r, peer):
        return pltpu.make_async_remote_copy(
            src_ref=src, dst_ref=dst, send_sem=s, recv_sem=r, device_id=peer, device_id_type=MESH
        )

    started = []

    def send(*args):
        remote(*args).start()

    def sent(buf, sem):
        started.append(remote(buf, buf, sem, sem, sib))

    def arrived(buf, sem):
        remote(buf, buf, sem, sem, sib).wait_recv()

    def nt(a, b):
        return lax.dot_general(a, b, (((1,), (1,)), ((), ())), preferred_element_type=F32)

    row = lax.broadcasted_iota(jnp.int32, (512, 384), 0)
    k = row & 15
    unit = ((row >> 4) & 7) * (NX * ROWS) + (row >> 7) * ROWS + k
    pick = (lax.broadcasted_iota(jnp.int32, (512, 384), 1) == unit) & (k < ROWS)
    pick = jnp.where(pick, 1.0, 0.0).astype(BF16)
    loads[0].wait()
    loads[1].wait()
    live = lax.broadcasted_iota(jnp.int32, (256, 384), 0) < cnt_ref[0]
    masked = jnp.where(live, go_ref[...].astype(F32), 0.0).astype(BF16)
    picked = nt(pick, masked)
    picked_t[...] = picked.astype(BF16).reshape(NX, 128, 256)
    units = picked.reshape(NX * NZ, 16, 256)
    blank = jnp.zeros((NX * NZ, 8, 256), F32)
    lhs[0] = jnp.concatenate([units, blank], axis=1).reshape(768, 256).astype(BF16).reshape(NX, 192, 256)
    moved = jnp.concatenate([blank, pltpu.roll(units[:, 8:16], 4, 1), units[:, 0:8]], axis=1)
    lhs[1] = moved.reshape(768, 256).astype(BF16).reshape(NX, 192, 256)

    def half(k, h):
        first = pl.multiple_of(WIDE * h, WIDE)
        out = nt(lhs[0, k], tok_ref[pl.ds(first, MAIN), :]) + nt(lhs[1, k], tok_ref[pl.ds(first + 512, MAIN), :])
        return out.reshape(NZ, 24, MAIN)

    def half_b(ref, h):
        first = pl.multiple_of(WIDE * h, WIDE)
        for k in range(NX):
            out = nt(lhs[0, k], tok_ref[pl.ds(first + MAIN, 128), :])
            out += nt(lhs[1, k], tok_ref[pl.ds(first + 512 + MAIN, 128), :])
            ref[:, k] = out.reshape(NZ, 24, 128)

    loads[2].wait()
    slabs = [(x + 2) % NX, (x + 1) % NX, (x + 3) % NX, x]

    def zat(d):
        return (z + d) % NZ

    def offer(j):
        k = slabs[j]
        other[k] = half(k, 1 - c)
        send(other.at[k], core_in.at[k], core_s.at[0], core_r.at[j], sib)

    def settle(j):
        k = slabs[j]
        arrived(core_in.at[k], core_r.at[j])
        acc[k] += core_in[k]

    def own(j):
        acc[slabs[j]] = half(slabs[j], c)

    halfway = ((4, 5, 6, 7), (3, 2, 1, 0))
    peer_of = (right, left)

    def skip(side, i):
        k = zat(halfway[side][i])
        if side == 0 and i % 2 == 0:
            arrived(core_in.at[0, 0:4], first_r.at[i // 2])
        acc[slabs[0], k] += core_in[slabs[0], k]
        send(acc.at[slabs[0], k], d2_in.at[side, i], d2_s, d2_r.at[side, i], peer_of[side])

    def step(side, d):
        k = zat(d)
        if d in halfway[side]:
            i = halfway[side].index(d)
            arrived(d2_in.at[side, i], d2_r.at[side, i])
            acc[slabs[1 + side], k] += d2_in[side, i]
        send(acc.at[slabs[1 + side], k], d1_in.at[side, d], d1_s, d1_r.at[d], peer_of[side])

    detour = tuple(jnp.where(c == 0, a, b) for a, b in zip(z_peers[1], z_peers[5]))
    detoured = jnp.where(c == 0, zat(2), zat(6))
    relays = {3: (z_peers[0], 0), 5: (z_peers[6], 1), 4: (detour, 2)}
    directs = {1: 0, 7: 1, 2: 2, 6: 3}

    def relay(block, d, buf, ss, rr):
        peer, slot = relays[d]
        send(block, buf.at[slot], ss, rr, peer)

    def direct(block, d, buf, ss, rr):
        slot = directs[d]
        send(block, buf.at[slot], ss, rr, z_peers[d - 1])

    def settle_x(d):
        arrived(d1_in.at[:, d], d1_r.at[d])
        acc[x, zat(d)] += d1_in[0, d] + d1_in[1, d]

    def deliver(d):
        settle_x(d)
        if d in relays:
            relay(acc.at[x, zat(d)], d, zm_in, zms, zmr)
        elif d:
            direct(acc.at[x, zat(d)], d, z_in, zs, zr)

    def deliver_mid():
        settle_x(2)
        settle_x(6)
        arrived(zm_in, zmr)
        for slot, to in enumerate((zat(2), zat(6), detoured)):
            acc[x, to] += zm_in[slot]
        for d in (2, 6):
            direct(acc.at[x, zat(d)], d, z_in, zs, zr)

    def deliver_mid_b():
        arrived(bm_in, bm_r)
        for slot, to in enumerate((zat(2), zat(6), detoured)):
            acc_b[to] += bm_in[slot]
        for d in (2, 6):
            direct(acc_b.at[zat(d)], d, bz_in, bz_s, bz_r)

    far_first = (4, 3, 5, 1, 7, 2, 6, 0)
    other[slabs[0]] = half(slabs[0], 1 - c)
    pl.semaphore_wait(barrier, len(everyone))
    for i in range(4):
        for side in range(2):
            k = zat(halfway[side][i])
            send(other.at[slabs[0], k], core_in.at[slabs[0], k], core_s.at[0], first_r.at[i // 2], sib)
    own(0)
    half_b(other_b, 1 - c)
    for d in far_first:
        send(other_b.at[zat(d)], core_b.at[zat(d)], bc_s, bc_r.at[0 if d in relays else 1], sib)
    for i in range(2):
        skip(0, i)
        skip(1, i)
    half_b(acc_b, c)
    for d in far_first:
        if d == far_first[0]:
            arrived(core_b.at[0:3], bc_r.at[0])
        if d == far_first[3]:
            arrived(core_b.at[0:5], bc_r.at[1])
        acc_b[zat(d)] += core_b[zat(d)]
        if d in relays:
            relay(acc_b.at[zat(d)], d, bm_in, bm_s, bm_r)
        elif d in (1, 7):
            direct(acc_b.at[zat(d)], d, bz_in, bz_s, bz_r)
    skip(0, 2)
    skip(1, 2)
    offer(1)
    offer(2)
    own(1)
    settle(1)
    step(0, 3)
    own(2)
    settle(2)
    step(1, 4)
    step(0, 4)
    step(1, 3)
    offer(3)
    rhs_t[...] = jnp.zeros_like(rhs_t)
    for k in range(NZ):
        for j in range(NX):
            lhs_t[16 * j : 16 * (j + 1), 256 * k : 256 * (k + 1)] = picked_t[j, 16 * k : 16 * (k + 1), :]
        for h in range(2):
            rhs_t[h, PART * k : PART * (k + 1), 256 * k : 256 * (k + 1)] = tok_ref[
                2 * WIDE + PART * h : 2 * WIDE + PART * (h + 1), :
            ]
    other_t[...] = nt(lhs_t[...], rhs_t[1 - c]).reshape(NX, 16, 128)
    send(other_t, core_t, core_s.at[1], core_r.at[0], sib)
    acc_t[...] = nt(lhs_t[...], rhs_t[c]).reshape(NX, 16, 128)
    own(3)
    settle(3)
    step(0, 5)
    step(1, 5)
    arrived(core_t, core_r.at[0])
    acc_t[...] += core_t[...]
    for d in range(1, NX):
        k = (x + d) % NX
        send(acc_t.at[k], xt_in.at[x], xts, xtr, x_peers[d - 1])
    skip(0, 3)
    step(1, 2)
    step(0, 2)
    skip(1, 3)
    deliver_mid_b()
    deliver(4)
    deliver(3)
    step(0, 6)
    step(1, 6)
    deliver(5)
    step(0, 1)
    step(1, 1)
    step(0, 7)
    step(1, 7)
    step(0, 0)
    step(1, 0)
    xt = acc_t[x]
    arrived(xt_in.at[0:3], xtr)
    for d in range(1, NX):
        xt += xt_in[(x + d) % NX]
    mine_t[...] = xt
    for d in range(1, NZ):
        send(mine_t, zt_in.at[z], zts, ztr, z_peers[d - 1])
    gathered = acc_b[z]
    arrived(bz_in, bz_r)
    for slot in range(4):
        gathered += bz_in[slot]
    acc_b[z] = gathered
    for d in range(1, NX):
        k = (x + d) % NX
        send(acc_b.at[z, k], bx_in.at[x], bx_s, bx_r, x_peers[d - 1])
    deliver(1)
    deliver(7)
    deliver_mid()
    deliver(0)
    for buf, sem in (
        (other, core_s.at[0]), (other_t, core_s.at[1]), (other_b, bc_s), (d2_in, d2_s), (d1_in, d1_s), (xt_in.at[0:3], xts),
        (zt_in.at[0:7], zts), (bm_in, bm_s), (bz_in, bz_s), (bx_in.at[0:3], bx_s), (zm_in, zms), (z_in, zs),
    ):
        sent(buf, sem)
    total_b = acc_b[z, x]
    arrived(bx_in.at[0:3], bx_r)
    for d in range(1, NX):
        total_b += bx_in[(x + d) % NX]
    total = acc[x, z]
    total_t = mine_t[...]
    arrived(zt_in.at[0:7], ztr)
    for d in (4, 5, 3, 6, 2, 7, 1):
        total_t += zt_in[zat(d)]
    arrived(z_in, zr)
    for slot in range(4):
        total += z_in[slot]
    total = jnp.concatenate([total, total_b], axis=1)

    lane = lax.broadcasted_iota(jnp.int32, (16, 128), 1)
    row = lax.broadcasted_iota(jnp.int32, (16, 128), 0)
    tail = jnp.where((row < ROWS) & (lane < PART), pltpu.roll(total_t, (8 - z) % 8 * PART, 1), 0.0)
    tail_up = jnp.where((row < ROWS) & (lane >= PART) & (lane < 2 * PART), pltpu.roll(total_t, (9 - z) % 8 * PART, 1), 0.0)
    g_own[...] = total
    gt_own[...] = tail

    for cp in loads[3:]:
        cp.wait()
    squared = total * total
    squared_t = tail * tail
    squared_up = tail_up * tail_up
    state = jnp.zeros((16, 128), F32)
    for k in range(OWN):
        state = jnp.where(jnp.where(row < ROWS, row, row - 4) == c * OWN + k, rs_ref[k], state)
    sums = jnp.sum(squared, axis=1, keepdims=True)
    sums_t = jnp.sum(squared_t, axis=1, keepdims=True)
    upper = jnp.broadcast_to(sums[8:16] + sums_t[8:16], (8, 128))
    r_own[0:8, :] = jnp.where(lane[0:8] < 64, sums[0:8] + sums[16:24] + sums_t[0:8], state[0:8])
    r_own[8:16, :] = jnp.where(lane[0:8] < 64, upper + pltpu.roll(upper, 4, 0), state[8:16])
    r_copy, g_copy, gt_copy = (
        remote(src, dst, gs.at[k], gr.at[k], sib)
        for k, (src, dst) in enumerate([(r_own, r_sib), (g_own, g_sib), (gt_own, gt_sib)])
    )
    for cp in (r_copy, g_copy, gt_copy):
        cp.start()
        started.append(cp)

    row24 = lax.broadcasted_iota(jnp.int32, (24, 1), 0)

    def columns(values, k):
        for h in range(2):
            part = jnp.sum(jnp.where((row24 < ROWS) == (h == 0), values, 0.0), axis=0, keepdims=True)
            for j in range(4):
                st_a[ma, k + 4 * h + j] = part[:, 128 * j : 128 * (j + 1)]

    ma = jnp.where(c == 0, e, z)
    mb = jnp.where(c == 0, z, e)
    columns(squared, 0)
    tail_c = jnp.sum(squared_t, axis=0, keepdims=True)
    r_copy.wait_recv()
    both = r_own[...] + r_sib[...]
    new_rows = 0.5 * both[:, 64:65] + 0.5 * (both[:, 0:1] / D + 1e-06)
    inverse = 1.0 / new_rows
    columns(squared * jnp.concatenate([inverse, inverse[0:8]], axis=0), 8)
    row_part = jnp.sum(jnp.where(row[:, 0:1] < ROWS, new_rows, 0.0), axis=0, keepdims=True)
    tail_s = jnp.sum(squared_up * inverse, axis=0, keepdims=True)
    st_a[ma, 16] = jnp.where(lane[0:1] < 2 * PART, tail_c + tail_s, row_part)

    def exchange(buf, me, s, r, peers):
        for d in (4, 3, 5, 2, 6, 1, 7):
            send(buf.at[me], buf.at[me], s, r, peers[d - 1])
        for cp in started:
            cp.wait_send()
        started.clear()
        sent(buf.at[0:7], s)
        arrived(buf.at[0:7], r)
        out = buf[0]
        for k in range(1, 8):
            out += buf[k]
        return out

    def either(a, b):
        return tuple(jnp.where(c == 0, i, j) for i, j in zip(a, b))

    st_b[mb] = exchange(st_a, ma, sas, sar, [either(a, b) for a, b in zip(y_peers, z_peers)])
    st_f[c, x] = exchange(st_b, mb, sbs, sbr, [either(b, a) for a, b in zip(y_peers, z_peers)])
    for d in (2, 1, 3):
        send(st_f.at[c, x], st_f.at[c, x], sfs, sfr, x_peers[d - 1])
        send(st_f.at[c, x], st_f.at[c, x], sfs, sfr, o_peers[d - 1])
    send(st_f.at[c, x], st_f.at[c, x], sfs, sfr, sib)
    for cp in started:
        cp.wait_send()
    started.clear()
    sent(st_a.at[0:7], sfs)

    def halves(own, sibling):
        return jnp.where(c == 0, own, sibling), jnp.where(c == 0, sibling, own)

    def rows_of(v, first):
        return jnp.where(c == 0, v[first : first + 6], v[first + 6 : first + 12])

    g_copy.wait_recv()
    gt_copy.wait_recv()
    low, high = halves(g_own[...], g_sib[...])
    for h in range(2):
        for first, v in ((512 * h, low), (WIDE + 512 * h, high)):
            v = jnp.concatenate([v[16:24], v[12:16]], axis=0) if h else v
            gwide[0:OWN, first : first + 512] = rows_of(v, 0)
    low, high = halves(gt_own[...], gt_sib[...])
    gwide[0:OWN, 2 * WIDE :] = rows_of(low + pltpu.roll(high, PART, 1), 0)
    rows6 = rows_of(new_rows, 0)
    gwide[0:OWN, :] *= lax.rsqrt(rows6)
    eye = lax.broadcasted_iota(jnp.int32, (OWN, 128), 0) == lax.broadcasted_iota(jnp.int32, (OWN, 128), 1)
    nr_ref[...] = jnp.sum(jnp.where(eye, rows6, 0.0), axis=0)[0:OWN]

    arrived(st_a.at[0:7], sfr)
    sums = []
    for cc in range(2):
        v = st_f[cc, 0]
        for k in range(1, NX):
            v += st_f[cc, k]
        sums.append(v)
    for cc in range(2):
        for j in range(2):
            for k in range(8):
                first = WIDE * cc + 128 * k
                wide[j : j + 1, first : first + 128] = sums[cc][8 * j + k]
    low, high = sums[0][16], sums[1][16]
    wide[0:1, 2 * WIDE :] = jnp.where(lane[0:1] < PART, low, pltpu.roll(high, PART, 1))
    wide[1:2, 2 * WIDE :] = jnp.where(lane[0:1] < PART, pltpu.roll(low, 128 - PART, 1), high)
    row_avg = sums[0][16][:, 2 * PART : 2 * PART + 1] / FFW
    new_cols = 0.5 * cs_ref[...].reshape(1, D) + 0.5 * (wide[0:1, 0:D] / FFW + 1e-06)
    nc_ref[...] = new_cols.reshape(D)
    total_sq = row_avg * jnp.sum(wide[1:2, 0:D] / new_cols, axis=1, keepdims=True)
    rms = jnp.sqrt(total_sq / (FFW * D))
    factor = 0.1 / jnp.maximum(1.0, rms) * jnp.sqrt(row_avg)
    scaled = gwide[0:OWN, 0:D] * (lax.rsqrt(new_cols) * factor)
    nw_ref[...] = (w_ref[...].astype(F32) - scaled).astype(BF16)

    for cp in started:
        cp.wait_send()


def store(a, b, c, a_out, b_out, c_out, sem):
    copies = [pltpu.make_async_copy(src, dst, sem.at[k]) for k, (src, dst) in enumerate([(a, a_out), (b, b_out), (c, c_out)])]
    for cp in copies:
        cp.start()
    for cp in copies:
        cp.wait()


def per_device(tokens, grad_out, counts, weight, row_state, col_state):
    vmem = pl.BlockSpec(memory_space=pltpu.VMEM)
    dma = pltpu.SemaphoreType.DMA

    def f32(*shape):
        return pltpu.VMEM(shape, F32)

    hbm = pl.BlockSpec(memory_space=pltpu.MemorySpace.HBM)
    results = (
        jax.ShapeDtypeStruct((OWN, D), BF16),
        jax.ShapeDtypeStruct((OWN,), F32),
        jax.ShapeDtypeStruct((D,), F32),
    )
    computed = pl.pallas_call(
        kernel,
        out_shape=tuple(pltpu.VMEM(r.shape, r.dtype) for r in results),
        in_specs=[hbm] * 6,
        out_specs=(vmem, vmem, vmem),
        scratch_shapes=[
            pltpu.VMEM((D, 256), BF16), pltpu.VMEM((256, 384), BF16), pltpu.SMEM((1,), jnp.int32),
            pltpu.VMEM((OWN, D), BF16), pltpu.SMEM((OWN,), F32), pltpu.VMEM((D,), F32), dma((6,)),
            pltpu.VMEM((2, NX, 192, 256), BF16),
            pltpu.VMEM((NX, 128, 256), BF16),
            pltpu.VMEM((64, 2048), BF16),
            pltpu.VMEM((2, 128, 2048), BF16),
            f32(NX, NZ, 24, MAIN), f32(NX, NZ, 24, MAIN), f32(NX, NZ, 24, MAIN),
            f32(NZ, NX, 24, 128), f32(NZ, NX, 24, 128), f32(NZ, NX, 24, 128), f32(4, NX, 24, 128), f32(3, NX, 24, 128), f32(NX, 24, 128),
            f32(NX, 16, 128), f32(NX, 16, 128), f32(NX, 16, 128),
            f32(2, 4, 24, MAIN), f32(2, NZ, 24, MAIN), f32(4, 24, MAIN), f32(3, 24, MAIN),
            f32(NX, 16, 128), f32(NZ, 16, 128), f32(16, 128),
            f32(*UNIT), f32(*UNIT), f32(16, 128), f32(16, 128), f32(16, 128), f32(16, 128),
            f32(8, STATS, 1, 128), f32(8, STATS, 1, 128), f32(2, NX, STATS, 1, 128),
            f32(8, 2 * WIDE + 128), f32(8, 2 * WIDE + 128),
            dma((2,)), dma((2,)), dma((4,)), dma(()), dma((2,)), dma(()), dma(()), dma(()), dma(()), dma(()), dma(()),
            dma(()), dma((2, 4)), dma(()), dma((8,)),
            dma(()), dma(()), dma(()), dma(()), dma(()), dma(()), dma(()), dma(()), dma((3,)), dma((3,)),
            dma(()), dma(()), dma(()), dma(()), dma(()), dma(()),
        ],
        compiler_params=pltpu.CompilerParams(
            collective_id=0, has_side_effects=True, vmem_limit_bytes=56 * 2**20
        ),
    )(tokens.T, grad_out, counts, weight, row_state, col_state)
    return pl.pallas_call(
        store,
        out_shape=results,
        in_specs=[vmem] * 3,
        out_specs=(hbm, hbm, hbm),
        scratch_shapes=[dma((3,))],
        compiler_params=pltpu.CompilerParams(vmem_limit_bytes=2**20),
    )(*computed)


def solution(mesh):
    placed = (
        P("dp", None),
        P("dp", "expert"),
        P("dp"),
        P(("expert", "dp"), None),
        P(("expert", "dp")),
        P(),
    )
    return jax.shard_map(
        per_device,
        mesh=mesh,
        in_specs=placed,
        out_specs=(P(("expert", "dp"), None), P(("expert", "dp")), P()),
        check_vma=False,
    )
```

```python
import jax
import jax.numpy as jnp
from jax import lax
from jax.experimental import pallas as pl
from jax.experimental.pallas import tpu as pltpu
from jax.sharding import PartitionSpec as P

D = 2080
FFW = 3072
NY, NZ, NX = 8, 8, 4
OWN = 6
ROWS = 12
WIDE = 1024
PART = 16
MAIN = 384
UNIT = (24, 512)
STATS = 17
MESH = pl.DeviceIdType.MESH
F32 = jnp.float32
BF16 = jnp.bfloat16


def kernel(
    tok_hbm, go_hbm, cnt_hbm, w_hbm, rs_hbm, cs_hbm,
    nw_ref, nr_ref, nc_ref,
    tok_ref, go_ref, cnt_ref, w_ref, rs_ref, cs_ref, in_s, lhs, picked, lhs_t, rhs_t, other, acc, core_in, other_b, acc_b, core_b, bz_in, bm_in, bx_in, other_t, acc_t, core_t, d2_in, d1_in, z_in, zm_in, xt_in, zt_in,
    mine_t, g_own, g_sib, gt_own, gt_sib, r_own, r_sib, st_a, st_b, st_f, wide, gwide,
    core_s, first_r, core_r, bc_s, bc_r, bz_s, bz_r, bm_s, bm_r, bx_s, bx_r, d2_s, d2_r, d1_s, d1_r,
    zs, zr, zms, zmr, xts, xtr, zts, ztr, gs, gr, sas, sar, sbs, sbr, sfs, sfr,
):
    e = lax.axis_index("expert")
    q = lax.axis_index("dp")
    c, x, z = q % 2, (q // 2) % NX, q // (2 * NX)

    def at(ee, zz, xx, cc):
        return (ee, (zz * NX + xx) * 2 + cc)

    sib = at(e, z, x, 1 - c)
    y_peers = [at((e + d) % NY, z, x, c) for d in range(1, NY)]
    z_peers = [at(e, (z + d) % NZ, x, c) for d in range(1, NZ)]
    x_peers = [at(e, z, (x + d) % NX, c) for d in range(1, NX)]
    o_peers = [at(e, z, (x + d) % NX, 1 - c) for d in range(1, NX)]
    right, left = x_peers[0], x_peers[2]

    loads = [
        pltpu.make_async_copy(src, dst, in_s.at[k])
        for k, (src, dst) in enumerate(
            [(cnt_hbm, cnt_ref), (go_hbm, go_ref), (tok_hbm, tok_ref), (rs_hbm, rs_ref), (cs_hbm, cs_ref), (w_hbm, w_ref)]
        )
    ]
    for cp in loads:
        cp.start()
    barrier = pltpu.get_barrier_semaphore()
    everyone = [sib] + y_peers + z_peers + x_peers + o_peers
    for peer in everyone:
        pl.semaphore_signal(barrier, inc=1, device_id=peer, device_id_type=MESH)

    def remote(src, dst, s, r, peer):
        return pltpu.make_async_remote_copy(
            src_ref=src, dst_ref=dst, send_sem=s, recv_sem=r, device_id=peer, device_id_type=MESH
        )

    started = []

    def send(*args):
        remote(*args).start()

    def sent(buf, sem):
        started.append(remote(buf, buf, sem, sem, sib))

    def arrived(buf, sem):
        remote(buf, buf, sem, sem, sib).wait_recv()

    def nt(a, b):
        return lax.dot_general(a, b, (((1,), (1,)), ((), ())), preferred_element_type=F32)

    row = lax.broadcasted_iota(jnp.int32, (512, 384), 0)
    k = row & 15
    unit = ((row >> 4) & 7) * (NX * ROWS) + (row >> 7) * ROWS + k
    pick = (lax.broadcasted_iota(jnp.int32, (512, 384), 1) == unit) & (k < ROWS)
    pick = jnp.where(pick, 1.0, 0.0).astype(BF16)
    loads[0].wait()
    loads[1].wait()
    live = lax.broadcasted_iota(jnp.int32, (256, 384), 0) < cnt_ref[0]
    masked = jnp.where(live, go_ref[...].astype(F32), 0.0).astype(BF16)
    picked[...] = nt(pick, masked).reshape(NX, 128, 256)

    def build(k):
        units = picked[k].reshape(NZ, 16, 256)
        blank = jnp.zeros((NZ, 8, 256), F32)
        lhs[0, k] = jnp.concatenate([units, blank], axis=1).reshape(192, 256).astype(BF16)
        moved = jnp.concatenate([blank, pltpu.roll(units[:, 8:16], 4, 1), units[:, 0:8]], axis=1)
        lhs[1, k] = moved.reshape(192, 256).astype(BF16)

    slabs = [(x + 2) % NX, (x + 1) % NX, (x + 3) % NX, x]
    build(slabs[0])

    def half(k, h):
        first = pl.multiple_of(WIDE * h, WIDE)
        out = nt(lhs[0, k], tok_ref[pl.ds(first, MAIN), :]) + nt(lhs[1, k], tok_ref[pl.ds(first + 512, MAIN), :])
        return out.reshape(NZ, 24, MAIN)

    def half_b(ref, h):
        first = pl.multiple_of(WIDE * h, WIDE)
        out = nt(lhs[0].reshape(768, 256), tok_ref[pl.ds(first + MAIN, 128), :])
        out += nt(lhs[1].reshape(768, 256), tok_ref[pl.ds(first + 512 + MAIN, 128), :])
        for k in range(NX):
            ref[:, k] = out[192 * k : 192 * (k + 1)].reshape(NZ, 24, 128)

    loads[2].wait()

    def zat(d):
        return (z + d) % NZ

    def offer(j):
        k = slabs[j]
        other[k] = half(k, 1 - c)
        send(other.at[k], core_in.at[k], core_s.at[0], core_r.at[j], sib)

    def settle(j):
        k = slabs[j]
        arrived(core_in.at[k], core_r.at[j])
        acc[k] += core_in[k]

    def own(j):
        acc[slabs[j]] = half(slabs[j], c)

    halfway = ((4, 5, 6, 7), (3, 2, 1, 0))
    peer_of = (right, left)

    def skip(side, i):
        k = zat(halfway[side][i])
        if side == 0 and i % 2 == 0:
            arrived(core_in.at[0, 0:4], first_r.at[i // 2])
        acc[slabs[0], k] += core_in[slabs[0], k]
        send(acc.at[slabs[0], k], d2_in.at[side, i], d2_s, d2_r.at[side, i], peer_of[side])

    def step(side, d):
        k = zat(d)
        if d in halfway[side]:
            i = halfway[side].index(d)
            arrived(d2_in.at[side, i], d2_r.at[side, i])
            acc[slabs[1 + side], k] += d2_in[side, i]
        send(acc.at[slabs[1 + side], k], d1_in.at[side, d], d1_s, d1_r.at[d], peer_of[side])

    detour = tuple(jnp.where(c == 0, a, b) for a, b in zip(z_peers[1], z_peers[5]))
    detoured = jnp.where(c == 0, zat(2), zat(6))
    relays = {3: (z_peers[0], 0), 5: (z_peers[6], 1), 4: (detour, 2)}
    directs = {1: 0, 7: 1, 2: 2, 6: 3}

    def relay(block, d, buf, ss, rr):
        peer, slot = relays[d]
        send(block, buf.at[slot], ss, rr, peer)

    def direct(block, d, buf, ss, rr):
        slot = directs[d]
        send(block, buf.at[slot], ss, rr, z_peers[d - 1])

    def settle_x(d):
        arrived(d1_in.at[:, d], d1_r.at[d])
        acc[x, zat(d)] += d1_in[0, d] + d1_in[1, d]

    def deliver(d):
        settle_x(d)
        if d in relays:
            relay(acc.at[x, zat(d)], d, zm_in, zms, zmr)
        elif d:
            direct(acc.at[x, zat(d)], d, z_in, zs, zr)

    def deliver_mid():
        settle_x(2)
        settle_x(6)
        arrived(zm_in, zmr)
        for slot, to in enumerate((zat(2), zat(6), detoured)):
            acc[x, to] += zm_in[slot]
        for d in (2, 6):
            direct(acc.at[x, zat(d)], d, z_in, zs, zr)

    def deliver_mid_b():
        arrived(bm_in, bm_r)
        for slot, to in enumerate((zat(2), zat(6), detoured)):
            acc_b[to] += bm_in[slot]
        for d in (2, 6):
            direct(acc_b.at[zat(d)], d, bz_in, bz_s, bz_r)

    far_first = (4, 3, 5, 1, 7, 2, 6, 0)
    other[slabs[0]] = half(slabs[0], 1 - c)
    pl.semaphore_wait(barrier, len(everyone))
    for i in range(4):
        for side in range(2):
            k = zat(halfway[side][i])
            send(other.at[slabs[0], k], core_in.at[slabs[0], k], core_s.at[0], first_r.at[i // 2], sib)
    own(0)
    for k in slabs[1:]:
        build(k)
    half_b(other_b, 1 - c)
    for d in far_first:
        send(other_b.at[zat(d)], core_b.at[zat(d)], bc_s, bc_r.at[0 if d in relays else 1], sib)
    for i in range(3):
        skip(0, i)
        skip(1, i)
    offer(1)
    offer(2)
    half_b(acc_b, c)
    for d in far_first:
        if d == far_first[0]:
            arrived(core_b.at[0:3], bc_r.at[0])
        if d == far_first[3]:
            arrived(core_b.at[0:5], bc_r.at[1])
        acc_b[zat(d)] += core_b[zat(d)]
        if d in relays:
            relay(acc_b.at[zat(d)], d, bm_in, bm_s, bm_r)
        elif d in (1, 7):
            direct(acc_b.at[zat(d)], d, bz_in, bz_s, bz_r)
    own(1)
    settle(1)
    step(0, 3)
    own(2)
    settle(2)
    step(1, 4)
    offer(3)
    step(0, 4)
    step(1, 3)
    step(0, 5)
    step(1, 5)
    skip(0, 3)
    skip(1, 3)
    step(1, 2)
    step(0, 2)
    rhs_t[...] = jnp.zeros_like(rhs_t)
    for k in range(NZ):
        for j in range(NX):
            lhs_t[16 * j : 16 * (j + 1), 256 * k : 256 * (k + 1)] = picked[j, 16 * k : 16 * (k + 1), :].astype(BF16)
        for h in range(2):
            rhs_t[h, PART * k : PART * (k + 1), 256 * k : 256 * (k + 1)] = tok_ref[
                2 * WIDE + PART * h : 2 * WIDE + PART * (h + 1), :
            ]
    other_t[...] = nt(lhs_t[...], rhs_t[1 - c]).reshape(NX, 16, 128)
    send(other_t, core_t, core_s.at[1], core_r.at[0], sib)
    acc_t[...] = nt(lhs_t[...], rhs_t[c]).reshape(NX, 16, 128)
    own(3)
    settle(3)
    arrived(core_t, core_r.at[0])
    acc_t[...] += core_t[...]
    for d in range(1, NX):
        k = (x + d) % NX
        send(acc_t.at[k], xt_in.at[x], xts, xtr, x_peers[d - 1])
    step(0, 6)
    step(1, 6)
    deliver_mid_b()
    deliver(4)
    deliver(3)
    step(0, 1)
    step(1, 1)
    deliver(5)
    step(0, 7)
    step(1, 7)
    step(0, 0)
    step(1, 0)
    xt = acc_t[x]
    arrived(xt_in.at[0:3], xtr)
    for d in range(1, NX):
        xt += xt_in[(x + d) % NX]
    mine_t[...] = xt
    for d in range(1, NZ):
        send(mine_t, zt_in.at[z], zts, ztr, z_peers[d - 1])
    gathered = acc_b[z]
    arrived(bz_in, bz_r)
    for slot in range(4):
        gathered += bz_in[slot]
    acc_b[z] = gathered
    for d in range(1, NX):
        k = (x + d) % NX
        send(acc_b.at[z, k], bx_in.at[x], bx_s, bx_r, x_peers[d - 1])
    deliver(1)
    deliver(7)
    deliver_mid()
    deliver(0)
    for buf, sem in (
        (other, core_s.at[0]), (other_t, core_s.at[1]), (other_b, bc_s), (d2_in, d2_s), (d1_in, d1_s), (xt_in.at[0:3], xts),
        (zt_in.at[0:7], zts), (bm_in, bm_s), (bz_in, bz_s), (bx_in.at[0:3], bx_s), (zm_in, zms), (z_in, zs),
    ):
        sent(buf, sem)
    total_b = acc_b[z, x]
    arrived(bx_in.at[0:3], bx_r)
    for d in range(1, NX):
        total_b += bx_in[(x + d) % NX]
    total = acc[x, z]
    total_t = mine_t[...]
    arrived(zt_in.at[0:7], ztr)
    for d in (4, 5, 3, 6, 2, 7, 1):
        total_t += zt_in[zat(d)]
    arrived(z_in, zr)
    for slot in range(4):
        total += z_in[slot]
    total = jnp.concatenate([total, total_b], axis=1)

    lane = lax.broadcasted_iota(jnp.int32, (16, 128), 1)
    row = lax.broadcasted_iota(jnp.int32, (16, 128), 0)
    tail = jnp.where((row < ROWS) & (lane < PART), pltpu.roll(total_t, (8 - z) % 8 * PART, 1), 0.0)
    tail_up = jnp.where((row < ROWS) & (lane >= PART) & (lane < 2 * PART), pltpu.roll(total_t, (9 - z) % 8 * PART, 1), 0.0)
    g_own[...] = total
    gt_own[...] = tail

    for cp in loads[3:]:
        cp.wait()
    squared = total * total
    squared_t = tail * tail
    squared_up = tail_up * tail_up
    state = jnp.zeros((16, 128), F32)
    for k in range(OWN):
        state = jnp.where(jnp.where(row < ROWS, row, row - 4) == c * OWN + k, rs_ref[k], state)
    sums = jnp.sum(squared, axis=1, keepdims=True)
    sums_t = jnp.sum(squared_t, axis=1, keepdims=True)
    upper = jnp.broadcast_to(sums[8:16] + sums_t[8:16], (8, 128))
    r_own[0:8, :] = jnp.where(lane[0:8] < 64, sums[0:8] + sums[16:24] + sums_t[0:8], state[0:8])
    r_own[8:16, :] = jnp.where(lane[0:8] < 64, upper + pltpu.roll(upper, 4, 0), state[8:16])
    r_copy, g_copy, gt_copy = (
        remote(src, dst, gs.at[k], gr.at[k], sib)
        for k, (src, dst) in enumerate([(r_own, r_sib), (g_own, g_sib), (gt_own, gt_sib)])
    )
    for cp in (r_copy, g_copy, gt_copy):
        cp.start()
        started.append(cp)

    row24 = lax.broadcasted_iota(jnp.int32, (24, 1), 0)

    def columns(values, k):
        for h in range(2):
            part = jnp.sum(jnp.where((row24 < ROWS) == (h == 0), values, 0.0), axis=0, keepdims=True)
            for j in range(4):
                st_a[ma, k + 4 * h + j] = part[:, 128 * j : 128 * (j + 1)]

    ma = jnp.where(c == 0, e, z)
    mb = jnp.where(c == 0, z, e)
    columns(squared, 0)
    tail_c = jnp.sum(squared_t, axis=0, keepdims=True)
    r_copy.wait_recv()
    both = r_own[...] + r_sib[...]
    new_rows = 0.5 * both[:, 64:65] + 0.5 * (both[:, 0:1] / D + 1e-06)
    inverse = 1.0 / new_rows
    columns(squared * jnp.concatenate([inverse, inverse[0:8]], axis=0), 8)
    row_part = jnp.sum(jnp.where(row[:, 0:1] < ROWS, new_rows, 0.0), axis=0, keepdims=True)
    tail_s = jnp.sum(squared_up * inverse, axis=0, keepdims=True)
    st_a[ma, 16] = jnp.where(lane[0:1] < 2 * PART, tail_c + tail_s, row_part)

    def exchange(buf, me, s, r, peers):
        for d in (4, 3, 5, 2, 6, 1, 7):
            send(buf.at[me], buf.at[me], s, r, peers[d - 1])
        for cp in started:
            cp.wait_send()
        started.clear()
        sent(buf.at[0:7], s)
        arrived(buf.at[0:7], r)
        out = buf[0]
        for k in range(1, 8):
            out += buf[k]
        return out

    def either(a, b):
        return tuple(jnp.where(c == 0, i, j) for i, j in zip(a, b))

    st_b[mb] = exchange(st_a, ma, sas, sar, [either(a, b) for a, b in zip(y_peers, z_peers)])
    st_f[c, x] = exchange(st_b, mb, sbs, sbr, [either(b, a) for a, b in zip(y_peers, z_peers)])
    for d in (2, 1, 3):
        send(st_f.at[c, x], st_f.at[c, x], sfs, sfr, x_peers[d - 1])
        send(st_f.at[c, x], st_f.at[c, x], sfs, sfr, o_peers[d - 1])
    send(st_f.at[c, x], st_f.at[c, x], sfs, sfr, sib)
    for cp in started:
        cp.wait_send()
    started.clear()
    sent(st_a.at[0:7], sfs)

    def halves(own, sibling):
        return jnp.where(c == 0, own, sibling), jnp.where(c == 0, sibling, own)

    def rows_of(v, first):
        return jnp.where(c == 0, v[first : first + 6], v[first + 6 : first + 12])

    g_copy.wait_recv()
    gt_copy.wait_recv()
    low, high = halves(g_own[...], g_sib[...])
    for h in range(2):
        for first, v in ((512 * h, low), (WIDE + 512 * h, high)):
            v = jnp.concatenate([v[16:24], v[12:16]], axis=0) if h else v
            gwide[0:OWN, first : first + 512] = rows_of(v, 0)
    low, high = halves(gt_own[...], gt_sib[...])
    gwide[0:OWN, 2 * WIDE :] = rows_of(low + pltpu.roll(high, PART, 1), 0)
    rows6 = rows_of(new_rows, 0)
    gwide[0:OWN, :] *= lax.rsqrt(rows6)
    eye = lax.broadcasted_iota(jnp.int32, (OWN, 128), 0) == lax.broadcasted_iota(jnp.int32, (OWN, 128), 1)
    nr_ref[...] = jnp.sum(jnp.where(eye, rows6, 0.0), axis=0)[0:OWN]

    arrived(st_a.at[0:7], sfr)
    sums = []
    for cc in range(2):
        v = st_f[cc, 0]
        for k in range(1, NX):
            v += st_f[cc, k]
        sums.append(v)
    for cc in range(2):
        for j in range(2):
            for k in range(8):
                first = WIDE * cc + 128 * k
                wide[j : j + 1, first : first + 128] = sums[cc][8 * j + k]
    low, high = sums[0][16], sums[1][16]
    wide[0:1, 2 * WIDE :] = jnp.where(lane[0:1] < PART, low, pltpu.roll(high, PART, 1))
    wide[1:2, 2 * WIDE :] = jnp.where(lane[0:1] < PART, pltpu.roll(low, 128 - PART, 1), high)
    row_avg = sums[0][16][:, 2 * PART : 2 * PART + 1] / FFW
    new_cols = 0.5 * cs_ref[...].reshape(1, D) + 0.5 * (wide[0:1, 0:D] / FFW + 1e-06)
    nc_ref[...] = new_cols.reshape(D)
    total_sq = row_avg * jnp.sum(wide[1:2, 0:D] / new_cols, axis=1, keepdims=True)
    rms = jnp.sqrt(total_sq / (FFW * D))
    factor = 0.1 / jnp.maximum(1.0, rms) * jnp.sqrt(row_avg)
    scaled = gwide[0:OWN, 0:D] * (lax.rsqrt(new_cols) * factor)
    nw_ref[...] = (w_ref[...].astype(F32) - scaled).astype(BF16)

    for cp in started:
        cp.wait_send()


def store(a, b, c, a_out, b_out, c_out, sem):
    copies = [pltpu.make_async_copy(src, dst, sem.at[k]) for k, (src, dst) in enumerate([(a, a_out), (b, b_out), (c, c_out)])]
    for cp in copies:
        cp.start()
    for cp in copies:
        cp.wait()


def per_device(tokens, grad_out, counts, weight, row_state, col_state):
    vmem = pl.BlockSpec(memory_space=pltpu.VMEM)
    dma = pltpu.SemaphoreType.DMA

    def f32(*shape):
        return pltpu.VMEM(shape, F32)

    hbm = pl.BlockSpec(memory_space=pltpu.MemorySpace.HBM)
    results = (
        jax.ShapeDtypeStruct((OWN, D), BF16),
        jax.ShapeDtypeStruct((OWN,), F32),
        jax.ShapeDtypeStruct((D,), F32),
    )
    computed = pl.pallas_call(
        kernel,
        out_shape=tuple(pltpu.VMEM(r.shape, r.dtype) for r in results),
        in_specs=[hbm] * 6,
        out_specs=(vmem, vmem, vmem),
        scratch_shapes=[
            pltpu.VMEM((D, 256), BF16), pltpu.VMEM((256, 384), BF16), pltpu.SMEM((1,), jnp.int32),
            pltpu.VMEM((OWN, D), BF16), pltpu.SMEM((OWN,), F32), pltpu.VMEM((D,), F32), dma((6,)),
            pltpu.VMEM((2, NX, 192, 256), BF16),
            f32(NX, 128, 256),
            pltpu.VMEM((64, 2048), BF16),
            pltpu.VMEM((2, 128, 2048), BF16),
            f32(NX, NZ, 24, MAIN), f32(NX, NZ, 24, MAIN), f32(NX, NZ, 24, MAIN),
            f32(NZ, NX, 24, 128), f32(NZ, NX, 24, 128), f32(NZ, NX, 24, 128), f32(4, NX, 24, 128), f32(3, NX, 24, 128), f32(NX, 24, 128),
            f32(NX, 16, 128), f32(NX, 16, 128), f32(NX, 16, 128),
            f32(2, 4, 24, MAIN), f32(2, NZ, 24, MAIN), f32(4, 24, MAIN), f32(3, 24, MAIN),
            f32(NX, 16, 128), f32(NZ, 16, 128), f32(16, 128),
            f32(*UNIT), f32(*UNIT), f32(16, 128), f32(16, 128), f32(16, 128), f32(16, 128),
            f32(8, STATS, 1, 128), f32(8, STATS, 1, 128), f32(2, NX, STATS, 1, 128),
            f32(8, 2 * WIDE + 128), f32(8, 2 * WIDE + 128),
            dma((2,)), dma((2,)), dma((4,)), dma(()), dma((2,)), dma(()), dma(()), dma(()), dma(()), dma(()), dma(()),
            dma(()), dma((2, 4)), dma(()), dma((8,)),
            dma(()), dma(()), dma(()), dma(()), dma(()), dma(()), dma(()), dma(()), dma((3,)), dma((3,)),
            dma(()), dma(()), dma(()), dma(()), dma(()), dma(()),
        ],
        compiler_params=pltpu.CompilerParams(
            collective_id=0, has_side_effects=True, vmem_limit_bytes=56 * 2**20
        ),
    )(tokens.T, grad_out, counts, weight, row_state, col_state)
    return pl.pallas_call(
        store,
        out_shape=results,
        in_specs=[vmem] * 3,
        out_specs=(hbm, hbm, hbm),
        scratch_shapes=[dma((3,))],
        compiler_params=pltpu.CompilerParams(vmem_limit_bytes=2**20),
    )(*computed)


def solution(mesh):
    placed = (
        P("dp", None),
        P("dp", "expert"),
        P("dp"),
        P(("expert", "dp"), None),
        P(("expert", "dp")),
        P(),
    )
    return jax.shard_map(
        per_device,
        mesh=mesh,
        in_specs=placed,
        out_specs=(P(("expert", "dp"), None), P(("expert", "dp")), P()),
        check_vma=False,
    )
```

```python
import jax
import jax.numpy as jnp
from jax import lax
from jax.experimental import pallas as pl
from jax.experimental.pallas import tpu as pltpu
from jax.sharding import PartitionSpec as P

D = 2080
FFW = 3072
NY, NZ, NX = 8, 8, 4
OWN = 6
ROWS = 12
WIDE = 1024
PART = 16
MAIN = 384
UNIT = (24, 512)
STATS = 17
MESH = pl.DeviceIdType.MESH
F32 = jnp.float32
BF16 = jnp.bfloat16


def kernel(
    tok_hbm, go_hbm, cnt_hbm, w_hbm, rs_hbm, cs_hbm,
    nw_ref, nr_ref, nc_ref,
    tok_ref, go_ref, cnt_ref, w_ref, rs_ref, cs_ref, in_s, lhs, picked, lhs_t, rhs_t, other, acc, core_in, other_b, acc_b, core_b, bz_in, bm_in, bx_in, other_t, acc_t, core_t, d2_in, d1_in, z_in, zm_in, xt_in, zt_in,
    mine_t, g_own, g_sib, gt_own, gt_sib, r_own, r_sib, st_a, st_b, st_f, wide, gwide,
    core_s, first_r, core_r, bc_s, bc_r, bz_s, bz_r, bm_s, bm_r, bx_s, bx_r, d2_s, d2_r, d1_s, d1_r,
    zs, zr, zms, zmr, xts, xtr, zts, ztr, gs, gr, sas, sar, sbs, sbr, sfs, sfr,
):
    e = lax.axis_index("expert")
    q = lax.axis_index("dp")
    c, x, z = q % 2, (q // 2) % NX, q // (2 * NX)

    def at(ee, zz, xx, cc):
        return (ee, (zz * NX + xx) * 2 + cc)

    sib = at(e, z, x, 1 - c)
    y_peers = [at((e + d) % NY, z, x, c) for d in range(1, NY)]
    z_peers = [at(e, (z + d) % NZ, x, c) for d in range(1, NZ)]
    x_peers = [at(e, z, (x + d) % NX, c) for d in range(1, NX)]
    o_peers = [at(e, z, (x + d) % NX, 1 - c) for d in range(1, NX)]
    right, left = x_peers[0], x_peers[2]

    loads = [
        pltpu.make_async_copy(src, dst, in_s.at[k])
        for k, (src, dst) in enumerate(
            [(cnt_hbm, cnt_ref), (go_hbm, go_ref), (tok_hbm, tok_ref), (rs_hbm, rs_ref), (cs_hbm, cs_ref), (w_hbm, w_ref)]
        )
    ]
    for cp in loads:
        cp.start()
    barrier = pltpu.get_barrier_semaphore()
    everyone = [p[d - 1] for d in (4, 3, 5, 2, 6, 1, 7) for p in (y_peers, z_peers)] + x_peers + o_peers + [sib]
    for peer in everyone:
        pl.semaphore_signal(barrier, inc=1, device_id=peer, device_id_type=MESH)

    def remote(src, dst, s, r, peer):
        return pltpu.make_async_remote_copy(
            src_ref=src, dst_ref=dst, send_sem=s, recv_sem=r, device_id=peer, device_id_type=MESH
        )

    started = []

    def send(*args):
        remote(*args).start()

    def sent(buf, sem):
        started.append(remote(buf, buf, sem, sem, sib))

    def arrived(buf, sem):
        remote(buf, buf, sem, sem, sib).wait_recv()

    def nt(a, b):
        return lax.dot_general(a, b, (((1,), (1,)), ((), ())), preferred_element_type=F32)

    row = lax.broadcasted_iota(jnp.int32, (512, 384), 0)
    k = row & 15
    unit = ((row >> 4) & 7) * (NX * ROWS) + (row >> 7) * ROWS + k
    pick = (lax.broadcasted_iota(jnp.int32, (512, 384), 1) == unit) & (k < ROWS)
    pick = jnp.where(pick, 1.0, 0.0).astype(BF16)
    loads[0].wait()
    loads[1].wait()
    live = lax.broadcasted_iota(jnp.int32, (256, 384), 0) < cnt_ref[0]
    masked = jnp.where(live, go_ref[...].astype(F32), 0.0).astype(BF16)
    picked[...] = nt(pick, masked).reshape(NX, 128, 256)

    def build(k):
        units = picked[k].reshape(NZ, 16, 256)
        blank = jnp.zeros((NZ, 8, 256), F32)
        lhs[0, k] = jnp.concatenate([units, blank], axis=1).reshape(192, 256).astype(BF16)
        moved = jnp.concatenate([blank, pltpu.roll(units[:, 8:16], 4, 1), units[:, 0:8]], axis=1)
        lhs[1, k] = moved.reshape(192, 256).astype(BF16)

    slabs = [(x + 2) % NX, (x + 1) % NX, (x + 3) % NX, x]
    build(slabs[0])

    def half(k, h):
        first = pl.multiple_of(WIDE * h, WIDE)
        out = nt(lhs[0, k], tok_ref[pl.ds(first, MAIN), :]) + nt(lhs[1, k], tok_ref[pl.ds(first + 512, MAIN), :])
        return out.reshape(NZ, 24, MAIN)

    def half_b(ref, h):
        first = pl.multiple_of(WIDE * h, WIDE)
        out = nt(lhs[0].reshape(768, 256), tok_ref[pl.ds(first + MAIN, 128), :])
        out += nt(lhs[1].reshape(768, 256), tok_ref[pl.ds(first + 512 + MAIN, 128), :])
        for k in range(NX):
            ref[:, k] = out[192 * k : 192 * (k + 1)].reshape(NZ, 24, 128)

    loads[2].wait()

    def zat(d):
        return (z + d) % NZ

    def offer(j):
        k = slabs[j]
        other[k] = half(k, 1 - c)
        send(other.at[k], core_in.at[k], core_s.at[0], core_r.at[j], sib)

    def settle(j):
        k = slabs[j]
        arrived(core_in.at[k], core_r.at[j])
        acc[k] += core_in[k]

    def own(j):
        acc[slabs[j]] = half(slabs[j], c)

    halfway = ((4, 5, 6, 7), (3, 2, 1, 0))
    peer_of = (right, left)

    def skip(side, i):
        k = zat(halfway[side][i])
        if side == 0 and i % 2 == 0:
            arrived(core_in.at[0, 0:4], first_r.at[i // 2])
        acc[slabs[0], k] += core_in[slabs[0], k]
        send(acc.at[slabs[0], k], d2_in.at[side, i], d2_s, d2_r.at[side, i], peer_of[side])

    def step(side, d):
        k = zat(d)
        if d in halfway[side]:
            i = halfway[side].index(d)
            arrived(d2_in.at[side, i], d2_r.at[side, i])
            acc[slabs[1 + side], k] += d2_in[side, i]
        send(acc.at[slabs[1 + side], k], d1_in.at[side, d], d1_s, d1_r.at[d], peer_of[side])

    detour = tuple(jnp.where(c == 0, a, b) for a, b in zip(z_peers[1], z_peers[5]))
    detoured = jnp.where(c == 0, zat(2), zat(6))
    relays = {3: (z_peers[0], 0), 5: (z_peers[6], 1), 4: (detour, 2)}
    directs = {1: 0, 7: 1, 2: 2, 6: 3}

    def relay(block, d, buf, ss, rr):
        peer, slot = relays[d]
        send(block, buf.at[slot], ss, rr, peer)

    def direct(block, d, buf, ss, rr):
        slot = directs[d]
        send(block, buf.at[slot], ss, rr, z_peers[d - 1])

    def settle_x(d):
        arrived(d1_in.at[:, d], d1_r.at[d])
        acc[x, zat(d)] += d1_in[0, d] + d1_in[1, d]

    def deliver(d):
        settle_x(d)
        if d in relays:
            relay(acc.at[x, zat(d)], d, zm_in, zms, zmr)
        elif d:
            direct(acc.at[x, zat(d)], d, z_in, zs, zr)

    def deliver_mid():
        settle_x(2)
        settle_x(6)
        arrived(zm_in, zmr)
        for slot, to in enumerate((zat(2), zat(6), detoured)):
            acc[x, to] += zm_in[slot]
        for d in (2, 6):
            direct(acc.at[x, zat(d)], d, z_in, zs, zr)

    def deliver_mid_b():
        arrived(bm_in, bm_r)
        for slot, to in enumerate((zat(2), zat(6), detoured)):
            acc_b[to] += bm_in[slot]
        for d in (2, 6):
            direct(acc_b.at[zat(d)], d, bz_in, bz_s, bz_r)

    far_first = (4, 3, 5, 1, 7, 2, 6, 0)
    other[slabs[0]] = half(slabs[0], 1 - c)
    pl.semaphore_wait(barrier, len(everyone))
    for i in range(4):
        for side in range(2):
            k = zat(halfway[side][i])
            send(other.at[slabs[0], k], core_in.at[slabs[0], k], core_s.at[0], first_r.at[i // 2], sib)
    own(0)
    for k in slabs[1:]:
        build(k)
    half_b(other_b, 1 - c)
    for d in far_first:
        send(other_b.at[zat(d)], core_b.at[zat(d)], bc_s, bc_r.at[0 if d in relays else 1], sib)
    for i in range(3):
        skip(0, i)
        skip(1, i)
    offer(1)
    offer(2)
    half_b(acc_b, c)
    for d in far_first:
        if d == far_first[0]:
            arrived(core_b.at[0:3], bc_r.at[0])
        if d == far_first[3]:
            arrived(core_b.at[0:5], bc_r.at[1])
        acc_b[zat(d)] += core_b[zat(d)]
        if d in relays:
            relay(acc_b.at[zat(d)], d, bm_in, bm_s, bm_r)
        elif d in (1, 7):
            direct(acc_b.at[zat(d)], d, bz_in, bz_s, bz_r)
    own(1)
    settle(1)
    step(0, 3)
    own(2)
    settle(2)
    step(1, 4)
    offer(3)
    step(0, 4)
    step(1, 3)
    step(0, 5)
    step(1, 5)
    skip(0, 3)
    skip(1, 3)
    step(1, 2)
    step(0, 2)
    rhs_t[...] = jnp.zeros_like(rhs_t)
    for k in range(NZ):
        for j in range(NX):
            lhs_t[16 * j : 16 * (j + 1), 256 * k : 256 * (k + 1)] = picked[j, 16 * k : 16 * (k + 1), :].astype(BF16)
        for h in range(2):
            rhs_t[h, PART * k : PART * (k + 1), 256 * k : 256 * (k + 1)] = tok_ref[
                2 * WIDE + PART * h : 2 * WIDE + PART * (h + 1), :
            ]
    other_t[...] = nt(lhs_t[...], rhs_t[1 - c]).reshape(NX, 16, 128)
    send(other_t, core_t, core_s.at[1], core_r.at[0], sib)
    acc_t[...] = nt(lhs_t[...], rhs_t[c]).reshape(NX, 16, 128)
    own(3)
    settle(3)
    arrived(core_t, core_r.at[0])
    acc_t[...] += core_t[...]
    for d in range(1, NX):
        k = (x + d) % NX
        send(acc_t.at[k], xt_in.at[x], xts, xtr, x_peers[d - 1])
    step(0, 6)
    step(1, 6)
    deliver_mid_b()
    deliver(4)
    deliver(3)
    step(0, 1)
    step(1, 1)
    deliver(5)
    step(0, 7)
    step(1, 7)
    step(0, 0)
    step(1, 0)
    xt = acc_t[x]
    arrived(xt_in.at[0:3], xtr)
    for d in range(1, NX):
        xt += xt_in[(x + d) % NX]
    mine_t[...] = xt
    for d in range(1, NZ):
        send(mine_t, zt_in.at[z], zts, ztr, z_peers[d - 1])
    deliver(1)
    deliver(7)
    gathered = acc_b[z]
    arrived(bz_in, bz_r)
    for slot in range(4):
        gathered += bz_in[slot]
    acc_b[z] = gathered
    for d in range(1, NX):
        k = (x + d) % NX
        send(acc_b.at[z, k], bx_in.at[x], bx_s, bx_r, x_peers[d - 1])
    deliver_mid()
    deliver(0)
    for buf, sem in (
        (other, core_s.at[0]), (other_t, core_s.at[1]), (other_b, bc_s), (d2_in, d2_s), (d1_in, d1_s), (xt_in.at[0:3], xts),
        (zt_in.at[0:7], zts), (bm_in, bm_s), (bz_in, bz_s), (bx_in.at[0:3], bx_s), (zm_in, zms), (z_in, zs),
    ):
        sent(buf, sem)
    total_b = acc_b[z, x]
    arrived(bx_in.at[0:3], bx_r)
    for d in range(1, NX):
        total_b += bx_in[(x + d) % NX]
    total = acc[x, z]
    total_t = mine_t[...]
    arrived(zt_in.at[0:7], ztr)
    for d in (4, 5, 3, 6, 2, 7, 1):
        total_t += zt_in[zat(d)]
    arrived(z_in, zr)
    for slot in range(4):
        total += z_in[slot]
    total = jnp.concatenate([total, total_b], axis=1)

    lane = lax.broadcasted_iota(jnp.int32, (16, 128), 1)
    row = lax.broadcasted_iota(jnp.int32, (16, 128), 0)
    tail = jnp.where((row < ROWS) & (lane < PART), pltpu.roll(total_t, (8 - z) % 8 * PART, 1), 0.0)
    tail_up = jnp.where((row < ROWS) & (lane >= PART) & (lane < 2 * PART), pltpu.roll(total_t, (9 - z) % 8 * PART, 1), 0.0)
    g_own[...] = total
    gt_own[...] = tail

    for cp in loads[3:]:
        cp.wait()
    squared = total * total
    squared_t = tail * tail
    squared_up = tail_up * tail_up
    state = jnp.zeros((16, 128), F32)
    for k in range(OWN):
        state = jnp.where(jnp.where(row < ROWS, row, row - 4) == c * OWN + k, rs_ref[k], state)
    sums = jnp.sum(squared, axis=1, keepdims=True)
    sums_t = jnp.sum(squared_t, axis=1, keepdims=True)
    upper = jnp.broadcast_to(sums[8:16] + sums_t[8:16], (8, 128))
    r_own[0:8, :] = jnp.where(lane[0:8] < 64, sums[0:8] + sums[16:24] + sums_t[0:8], state[0:8])
    r_own[8:16, :] = jnp.where(lane[0:8] < 64, upper + pltpu.roll(upper, 4, 0), state[8:16])
    r_copy, g_copy, gt_copy = (
        remote(src, dst, gs.at[k], gr.at[k], sib)
        for k, (src, dst) in enumerate([(r_own, r_sib), (g_own, g_sib), (gt_own, gt_sib)])
    )
    for cp in (r_copy, g_copy, gt_copy):
        cp.start()
        started.append(cp)

    row24 = lax.broadcasted_iota(jnp.int32, (24, 1), 0)

    def columns(values, k):
        for h in range(2):
            part = jnp.sum(jnp.where((row24 < ROWS) == (h == 0), values, 0.0), axis=0, keepdims=True)
            for j in range(4):
                st_a[ma, k + 4 * h + j] = part[:, 128 * j : 128 * (j + 1)]

    ma = jnp.where(c == 0, e, z)
    mb = jnp.where(c == 0, z, e)
    columns(squared, 0)
    tail_c = jnp.sum(squared_t, axis=0, keepdims=True)
    r_copy.wait_recv()
    both = r_own[...] + r_sib[...]
    new_rows = 0.5 * both[:, 64:65] + 0.5 * (both[:, 0:1] / D + 1e-06)
    inverse = 1.0 / new_rows
    columns(squared * jnp.concatenate([inverse, inverse[0:8]], axis=0), 8)
    row_part = jnp.sum(jnp.where(row[:, 0:1] < ROWS, new_rows, 0.0), axis=0, keepdims=True)
    tail_s = jnp.sum(squared_up * inverse, axis=0, keepdims=True)
    st_a[ma, 16] = jnp.where(lane[0:1] < 2 * PART, tail_c + tail_s, row_part)

    def exchange(buf, me, s, r, peers):
        for d in (4, 3, 5, 2, 6, 1, 7):
            send(buf.at[me], buf.at[me], s, r, peers[d - 1])
        for cp in started:
            cp.wait_send()
        started.clear()
        sent(buf.at[0:7], s)
        arrived(buf.at[0:7], r)
        out = buf[0]
        for k in range(1, 8):
            out += buf[k]
        return out

    def either(a, b):
        return tuple(jnp.where(c == 0, i, j) for i, j in zip(a, b))

    st_b[mb] = exchange(st_a, ma, sas, sar, [either(a, b) for a, b in zip(y_peers, z_peers)])
    st_f[c, x] = exchange(st_b, mb, sbs, sbr, [either(b, a) for a, b in zip(y_peers, z_peers)])
    for d in (2, 1, 3):
        send(st_f.at[c, x], st_f.at[c, x], sfs, sfr, x_peers[d - 1])
        send(st_f.at[c, x], st_f.at[c, x], sfs, sfr, o_peers[d - 1])
    send(st_f.at[c, x], st_f.at[c, x], sfs, sfr, sib)
    for cp in started:
        cp.wait_send()
    started.clear()
    sent(st_a.at[0:7], sfs)

    def halves(own, sibling):
        return jnp.where(c == 0, own, sibling), jnp.where(c == 0, sibling, own)

    def rows_of(v, first):
        return jnp.where(c == 0, v[first : first + 6], v[first + 6 : first + 12])

    g_copy.wait_recv()
    gt_copy.wait_recv()
    low, high = halves(g_own[...], g_sib[...])
    for h in range(2):
        for first, v in ((512 * h, low), (WIDE + 512 * h, high)):
            v = jnp.concatenate([v[16:24], v[12:16]], axis=0) if h else v
            gwide[0:OWN, first : first + 512] = rows_of(v, 0)
    low, high = halves(gt_own[...], gt_sib[...])
    gwide[0:OWN, 2 * WIDE :] = rows_of(low + pltpu.roll(high, PART, 1), 0)
    rows6 = rows_of(new_rows, 0)
    gwide[0:OWN, :] *= lax.rsqrt(rows6)
    eye = lax.broadcasted_iota(jnp.int32, (OWN, 128), 0) == lax.broadcasted_iota(jnp.int32, (OWN, 128), 1)
    nr_ref[...] = jnp.sum(jnp.where(eye, rows6, 0.0), axis=0)[0:OWN]

    arrived(st_a.at[0:7], sfr)
    sums = []
    for cc in range(2):
        v = st_f[cc, 0]
        for k in range(1, NX):
            v += st_f[cc, k]
        sums.append(v)
    for cc in range(2):
        for j in range(2):
            for k in range(8):
                first = WIDE * cc + 128 * k
                wide[j : j + 1, first : first + 128] = sums[cc][8 * j + k]
    low, high = sums[0][16], sums[1][16]
    wide[0:1, 2 * WIDE :] = jnp.where(lane[0:1] < PART, low, pltpu.roll(high, PART, 1))
    wide[1:2, 2 * WIDE :] = jnp.where(lane[0:1] < PART, pltpu.roll(low, 128 - PART, 1), high)
    row_avg = sums[0][16][:, 2 * PART : 2 * PART + 1] / FFW
    new_cols = 0.5 * cs_ref[...].reshape(1, D) + 0.5 * (wide[0:1, 0:D] / FFW + 1e-06)
    nc_ref[...] = new_cols.reshape(D)
    total_sq = row_avg * jnp.sum(wide[1:2, 0:D] / new_cols, axis=1, keepdims=True)
    rms = jnp.sqrt(total_sq / (FFW * D))
    factor = 0.1 / jnp.maximum(1.0, rms) * jnp.sqrt(row_avg)
    scaled = gwide[0:OWN, 0:D] * (lax.rsqrt(new_cols) * factor)
    nw_ref[...] = (w_ref[...].astype(F32) - scaled).astype(BF16)

    for cp in started:
        cp.wait_send()


def store(a, b, c, a_out, b_out, c_out, sem):
    copies = [pltpu.make_async_copy(src, dst, sem.at[k]) for k, (src, dst) in enumerate([(a, a_out), (b, b_out), (c, c_out)])]
    for cp in copies:
        cp.start()
    for cp in copies:
        cp.wait()


def per_device(tokens, grad_out, counts, weight, row_state, col_state):
    vmem = pl.BlockSpec(memory_space=pltpu.VMEM)
    dma = pltpu.SemaphoreType.DMA

    def f32(*shape):
        return pltpu.VMEM(shape, F32)

    hbm = pl.BlockSpec(memory_space=pltpu.MemorySpace.HBM)
    results = (
        jax.ShapeDtypeStruct((OWN, D), BF16),
        jax.ShapeDtypeStruct((OWN,), F32),
        jax.ShapeDtypeStruct((D,), F32),
    )
    computed = pl.pallas_call(
        kernel,
        out_shape=tuple(pltpu.VMEM(r.shape, r.dtype) for r in results),
        in_specs=[hbm] * 6,
        out_specs=(vmem, vmem, vmem),
        scratch_shapes=[
            pltpu.VMEM((D, 256), BF16), pltpu.VMEM((256, 384), BF16), pltpu.SMEM((1,), jnp.int32),
            pltpu.VMEM((OWN, D), BF16), pltpu.SMEM((OWN,), F32), pltpu.VMEM((D,), F32), dma((6,)),
            pltpu.VMEM((2, NX, 192, 256), BF16),
            f32(NX, 128, 256),
            pltpu.VMEM((64, 2048), BF16),
            pltpu.VMEM((2, 128, 2048), BF16),
            f32(NX, NZ, 24, MAIN), f32(NX, NZ, 24, MAIN), f32(NX, NZ, 24, MAIN),
            f32(NZ, NX, 24, 128), f32(NZ, NX, 24, 128), f32(NZ, NX, 24, 128), f32(4, NX, 24, 128), f32(3, NX, 24, 128), f32(NX, 24, 128),
            f32(NX, 16, 128), f32(NX, 16, 128), f32(NX, 16, 128),
            f32(2, 4, 24, MAIN), f32(2, NZ, 24, MAIN), f32(4, 24, MAIN), f32(3, 24, MAIN),
            f32(NX, 16, 128), f32(NZ, 16, 128), f32(16, 128),
            f32(*UNIT), f32(*UNIT), f32(16, 128), f32(16, 128), f32(16, 128), f32(16, 128),
            f32(8, STATS, 1, 128), f32(8, STATS, 1, 128), f32(2, NX, STATS, 1, 128),
            f32(8, 2 * WIDE + 128), f32(8, 2 * WIDE + 128),
            dma((2,)), dma((2,)), dma((4,)), dma(()), dma((2,)), dma(()), dma(()), dma(()), dma(()), dma(()), dma(()),
            dma(()), dma((2, 4)), dma(()), dma((8,)),
            dma(()), dma(()), dma(()), dma(()), dma(()), dma(()), dma(()), dma(()), dma((3,)), dma((3,)),
            dma(()), dma(()), dma(()), dma(()), dma(()), dma(()),
        ],
        compiler_params=pltpu.CompilerParams(
            collective_id=0, has_side_effects=True, vmem_limit_bytes=56 * 2**20
        ),
    )(tokens.T, grad_out, counts, weight, row_state, col_state)
    return pl.pallas_call(
        store,
        out_shape=results,
        in_specs=[vmem] * 3,
        out_specs=(hbm, hbm, hbm),
        scratch_shapes=[dma((3,))],
        compiler_params=pltpu.CompilerParams(vmem_limit_bytes=2**20),
    )(*computed)


def solution(mesh):
    placed = (
        P("dp", None),
        P("dp", "expert"),
        P("dp"),
        P(("expert", "dp"), None),
        P(("expert", "dp")),
        P(),
    )
    return jax.shard_map(
        per_device,
        mesh=mesh,
        in_specs=placed,
        out_specs=(P(("expert", "dp"), None), P(("expert", "dp")), P()),
        check_vma=False,
    )
```
